32 devices in a mesh: pipe: 8 (over y, x, core), fsdp: 4 (over z).
Axes of the slice: x: 2, y: 2, z: 4, core: 2. Of those that a mesh axis runs over, the one named last changes fastest.
Arguments:
- handoff_gradient: bfloat16 [8, 768, 8192], P('pipe', 'fsdp'), may hold values from -12 to 12
- output_weight: bfloat16 [8, 8192, 8192], P('pipe', 'fsdp'), may hold values from -0.0625 to 0.0625
- adapter_down: bfloat16 [8, 16, 8192], P('pipe', None, 'fsdp'), may hold values from -0.0625 to 0.0625
- adapter_up: bfloat16 [8, 16, 8192], P('pipe', None, 'fsdp'), may hold values from -0.29882812 to 0.29882812
- stored_queries: bfloat16 [8, 768, 8192], P('pipe', None, 'fsdp'), may hold values from -64 to 64
- stored_keys: bfloat16 [8, 768, 1024], P('pipe', None, 'fsdp'), may hold values from -3 to 3
- stored_values: bfloat16 [8, 768, 1024], P('pipe', None, 'fsdp'), may hold values from -6 to 6
- segments: int32 [8, 768], P('pipe'), may hold values from 0 to 7, never falling along the last dimension, each value on 1 to 384 neighbouring positions
Outputs:
- query_gradient: bfloat16 [8, 768, 8192], P('pipe', None, 'fsdp')
- key_gradient: bfloat16 [8, 768, 1024], P('pipe', None, 'fsdp')
- value_gradient: bfloat16 [8, 768, 1024], P('pipe', None, 'fsdp')
- down_map_gradient: float32 [8, 16, 8192], P('pipe', None, 'fsdp')
- up_map_gradient: float32 [8, 16, 8192], P('pipe', None, 'fsdp')
The draws below stay inside these ranges and needn't reach their ends.
Inputs may be any that keep to these rules, and one draw needn't show every extreme that they name: `segments`: ids never fall along a micro-batch.
All inputs are finite; a program needn't handle non-finite values.
Results may differ from the reference program's by a relative error of at most 0.015.
The reference program's roundings to bfloat16 on the way count: a program that leaves them out, or rounds other values in their place, can miss the bound.
Values may be sent and summed in bfloat16 or wider, within the bound.
No kernel may reach another device: no remote copies, remote signals or barrier semaphores. Data moves between devices by JAX's collectives and lax.ppermute only.
A program may use at most 128 MiB of HBM per device.

```python
import math
import jax
import jax.numpy as jnp
import numpy as np
from jax import lax

MODEL_WIDTH = 8192
QUERY_HEADS = 64
VALUE_HEADS = 8
HEAD_SIZE = 128
ADAPTER_RANK = 16
DOCS = 8
MICRO_TOKENS = 768
N_PIPE = 8


def paired_draws(key):
    random_key_split = jax.random.fold_in(key, 101)
    key_queries = jax.random.fold_in(key, 202)
    random_key_draw = jnp.clip(jax.random.normal(random_key_split, (N_PIPE, MICRO_TOKENS, VALUE_HEADS, HEAD_SIZE), jnp.float32), -3.0, 3.0)
    query_rows = jnp.clip(jax.random.normal(key_queries, (N_PIPE, MICRO_TOKENS, QUERY_HEADS, HEAD_SIZE), jnp.float32), -4.0, 4.0)
    return (query_rows.reshape(N_PIPE, MICRO_TOKENS, QUERY_HEADS * HEAD_SIZE), random_key_draw.reshape(N_PIPE, MICRO_TOKENS, VALUE_HEADS * HEAD_SIZE))


def draw_stored_queries(key, part):
    return paired_draws(key)[0].astype(jnp.bfloat16)


def draw_stored_keys(key, part):
    return paired_draws(key)[1].astype(jnp.bfloat16)


def steps_of(own_key, extent, split, smallest, largest):
    def one(position, shards_of):
        draws = jax.random.uniform(jax.random.fold_in(jax.random.fold_in(own_key, 6), position), (shards_of,), jnp.float32, smallest / len(split), largest / len(split))
        return jnp.repeat(jnp.exp(draws), extent[position] // shards_of).reshape((-1,) + (1,) * (len(extent) - position - 1))

    gain = one(*split[0])
    for cut in split[1:]:
        gain = gain * one(*cut)
    return gain


def profile(amount, total, most, lean):
    weights = [(1 << 20) // math.isqrt(standing ** lean) + 1 for standing in range(2, amount + 1)]
    surplus, counts = total - most - (amount - 1), [1] * (amount - 1)
    while surplus > 0:
        free = [i for i in range(amount - 1) if counts[i] < most]
        pool, left = sum([weights[i] for i in free]), surplus
        for i in free:
            more = min(most - counts[i], max(1, left * weights[i] // pool), surplus)
            counts[i] = counts[i] + more
            surplus = surplus - more
    return np.array([most] + counts)


def ragged(key, amount, total, bound, skew):
    if amount == 2:
        one = jax.random.randint(key, (), max(1, total - bound), min(bound, total - 1) + 1)
        return jnp.stack([one, total - one])
    tallies = jnp.asarray(profile(amount, total, bound, skew), jnp.int32)
    couples = (amount - 1) // 2
    giver, sink = tallies[1:1 + 2 * couples:2], tallies[2:2 + 2 * couples:2]
    room = jnp.minimum(giver - 1, bound - sink)
    passed = jax.random.randint(jax.random.fold_in(key, 1), (couples,), 0, 1 << 20) % (room + 1)
    tallies = tallies.at[1:1 + 2 * couples:2].set(giver - passed).at[2:2 + 2 * couples:2].set(sink + passed)
    return tallies[jax.random.permutation(jax.random.fold_in(key, 2), amount)]


def bell_draw(own_key, extent, spread, most, shards=(), held_as=jnp.bfloat16):
    drawn = spread * jax.random.normal(own_key, extent, jnp.float32)
    if shards:
        drawn = drawn * steps_of(own_key, extent, shards, -0.22, 0.18)
    return jnp.clip(drawn, -most, most).astype(held_as)


def setup_inputs(seed: int = 0) -> dict:
    key_list = jax.random.split(jax.random.key(seed), 9)
    handoff_gradient = bell_draw(key_list[0], (N_PIPE, MICRO_TOKENS, MODEL_WIDTH), 2.0, 12.0, ((0, 8), (1, 4)))
    output_weight = bell_draw(key_list[1], (N_PIPE, QUERY_HEADS * HEAD_SIZE, MODEL_WIDTH), MODEL_WIDTH ** -0.5, 0.0625, ((0, 8), (1, 4)))
    adapter_down = bell_draw(key_list[2], (N_PIPE, ADAPTER_RANK, QUERY_HEADS * HEAD_SIZE), (QUERY_HEADS * HEAD_SIZE) ** -0.5, 0.0625, ((0, 8), (2, 4)))
    adapter_up = bell_draw(key_list[3], (N_PIPE, ADAPTER_RANK, MODEL_WIDTH), 0.05, 0.29882812, ((0, 8), (2, 4)))
    stored_queries = draw_stored_queries(jax.random.fold_in(key_list[8], 71), 0)
    stored_keys = draw_stored_keys(jax.random.fold_in(key_list[8], 71), 0)
    stored_values = bell_draw(key_list[6], (N_PIPE, MICRO_TOKENS, VALUE_HEADS * HEAD_SIZE), 1.0, 6.0, ((0, 8), (2, 4)))
    segments = jax.vmap(lambda own: jnp.searchsorted(jnp.cumsum(ragged(own, DOCS, MICRO_TOKENS, MICRO_TOKENS // 2, 1)), jnp.arange(MICRO_TOKENS), side="right"))(jax.random.split(key_list[7], N_PIPE)).reshape((N_PIPE, MICRO_TOKENS)).astype(jnp.int32)
    return {"handoff_gradient": handoff_gradient, "output_weight": output_weight, "adapter_down": adapter_down, "adapter_up": adapter_up, "stored_queries": stored_queries, "stored_keys": stored_keys, "stored_values": stored_values, "segments": segments}


adapter_scale = 2.0

def attend(query_block, key_head, value_head, context_gradient, allowed):
    inv_scale = 1.0 / math.sqrt(query_block.shape[-1])
    scores = jnp.einsum('bngd,snd->ngbs', query_block.astype(jnp.float32), key_head.astype(jnp.float32)) * inv_scale
    scores = jnp.where(allowed[None, None], scores, -jnp.inf)
    row_max = lax.optimization_barrier(jnp.max(scores, axis=-1, keepdims=True))
    expanded = jnp.exp(scores - row_max)
    attn_probs = expanded / lax.optimization_barrier(jnp.sum(expanded, axis=-1, keepdims=True))
    probs_low = lax.optimization_barrier(attn_probs.astype(jnp.bfloat16))
    context_rows = jnp.einsum('ngbs,snd->bngd', probs_low.astype(jnp.float32), value_head.astype(jnp.float32))
    context_rows = lax.optimization_barrier(context_rows.astype(jnp.bfloat16))
    grad_probs = jnp.einsum('bngd,snd->ngbs', context_gradient.astype(jnp.float32), value_head.astype(jnp.float32))
    row_delta = lax.optimization_barrier(jnp.sum(context_gradient.astype(jnp.float32) * context_rows.astype(jnp.float32), axis=-1))
    row_delta = jnp.transpose(row_delta, (1, 2, 0))[..., None]
    grad_scores = lax.optimization_barrier((attn_probs * (grad_probs - row_delta)).astype(jnp.bfloat16))
    grad_query = jnp.einsum('ngbs,snd->bngd', grad_scores.astype(jnp.float32), key_head.astype(jnp.float32))
    grad_query = (grad_query * inv_scale).astype(jnp.bfloat16)
    gradient_of_key = jnp.einsum('ngbs,bngd->snd', grad_scores.astype(jnp.float32), query_block.astype(jnp.float32)) * inv_scale
    gradient_of_value = jnp.einsum('ngbs,bngd->snd', probs_low.astype(jnp.float32), context_gradient.astype(jnp.float32))
    return (context_rows, grad_query, gradient_of_key, gradient_of_value)

def reference(handoff_gradient, output_weight, adapter_down, adapter_up, stored_queries, stored_keys, stored_values, segments):
    query_group_count = QUERY_HEADS // VALUE_HEADS
    positions = jnp.arange(MICRO_TOKENS)
    causal = positions[None, :] <= positions[:, None]
    result_list = ([], [], [], [], [])
    for section_number in range(N_PIPE):
        incoming_gradient = handoff_gradient[(section_number + 1) % N_PIPE]
        source_section = N_PIPE - 1 - section_number
        doc_ids = segments[section_number]
        allowed = causal & (doc_ids[:, None] == doc_ids[None, :])
        rank_gradient = jnp.dot(incoming_gradient, adapter_up[section_number].T, preferred_element_type=jnp.float32)
        frozen_portion = jnp.dot(incoming_gradient, output_weight[section_number].T, preferred_element_type=jnp.float32)
        rank_projected = jnp.dot(rank_gradient, adapter_down[section_number].astype(jnp.float32), precision=lax.Precision.HIGHEST)
        context_gradient = lax.optimization_barrier((frozen_portion + adapter_scale * rank_projected).astype(jnp.bfloat16))
        query_head_rows = stored_queries[source_section].reshape(MICRO_TOKENS, VALUE_HEADS, query_group_count, HEAD_SIZE).transpose(1, 0, 2, 3)[:, :, None]
        gradient_per_head = context_gradient.reshape(MICRO_TOKENS, VALUE_HEADS, query_group_count, HEAD_SIZE).transpose(1, 0, 2, 3)[:, :, None]
        key_head_rows = stored_keys[source_section].reshape(MICRO_TOKENS, VALUE_HEADS, HEAD_SIZE).transpose(1, 0, 2)[:, :, None]
        value_head_rows = stored_values[source_section].reshape(MICRO_TOKENS, VALUE_HEADS, HEAD_SIZE).transpose(1, 0, 2)[:, :, None]

        def one_head(head_items):
            return attend(head_items[0], head_items[1], head_items[2], head_items[3], allowed)
        context_rows, grad_query, gradient_of_key, gradient_of_value = lax.map(one_head, (query_head_rows, key_head_rows, value_head_rows, gradient_per_head))
        context_rows = context_rows.transpose(1, 0, 2, 3, 4).reshape(MICRO_TOKENS, QUERY_HEADS * HEAD_SIZE)
        grad_query = grad_query.transpose(1, 0, 2, 3, 4).reshape(MICRO_TOKENS, QUERY_HEADS * HEAD_SIZE)
        gradient_of_key = gradient_of_key.transpose(1, 0, 2, 3).reshape(MICRO_TOKENS, VALUE_HEADS * HEAD_SIZE).astype(jnp.bfloat16)
        gradient_of_value = gradient_of_value.transpose(1, 0, 2, 3).reshape(MICRO_TOKENS, VALUE_HEADS * HEAD_SIZE).astype(jnp.bfloat16)
        rank_context = jnp.dot(context_rows, adapter_down[section_number].T, preferred_element_type=jnp.float32)
        gradient_scale = adapter_scale / math.sqrt(MICRO_TOKENS)
        adapter_down_gradient = gradient_scale * jnp.dot(rank_gradient.T, context_rows.astype(jnp.float32), precision=lax.Precision.HIGHEST)
        adapter_up_gradient = gradient_scale * jnp.dot(rank_context.T, incoming_gradient.astype(jnp.float32), precision=lax.Precision.HIGHEST)
        result_list[0].append(grad_query)
        result_list[1].append(gradient_of_key)
        result_list[2].append(gradient_of_value)
        result_list[3].append(adapter_down_gradient)
        result_list[4].append(adapter_up_gradient)
    return (jnp.stack(result_list[0]), jnp.stack(result_list[1]), jnp.stack(result_list[2]), jnp.stack(result_list[3]), jnp.stack(result_list[4]))
```

```python
import functools
import math

import jax
import jax.numpy as jnp
from jax import lax
from jax.experimental import pallas as pl
from jax.experimental.pallas import tpu as pltpu
from jax.sharding import PartitionSpec as P

HEAD_SIZE = 128
DOC_REACH = 384
MASKED = -1e30
LOG2E = math.log2(math.e)
VMEM_BYTES = 44 * 2**20

adapter_scale = 2.0


def dot_nt(a, b):
    return lax.dot_general(a, b, (((1,), (1,)), ((), ())), preferred_element_type=jnp.float32)


def dot_nn(a, b):
    return lax.dot_general(a, b, (((1,), (0,)), ((), ())), preferred_element_type=jnp.float32)


def dot_tn(a, b):
    return lax.dot_general(a, b, (((0,), (0,)), ((), ())), preferred_element_type=jnp.float32)


def three_parts(a):
    high = a.astype(jnp.bfloat16)
    rest = a - high.astype(jnp.float32)
    middle = rest.astype(jnp.bfloat16)
    low = (rest - middle.astype(jnp.float32)).astype(jnp.bfloat16)
    return jnp.concatenate([high, middle, low], axis=0)


def folded(a):
    rows = a.shape[0] // 3
    return a[:rows] + a[rows : 2 * rows] + a[2 * rows :]


def stacked_heads(a):
    count = a.shape[1] // HEAD_SIZE
    return jnp.concatenate(
        [a[:, h * HEAD_SIZE : (h + 1) * HEAD_SIZE] for h in range(count)], axis=0
    )


def mask_bias(key_start, key_ids, query_pos, query_ids, shape):
    key_pos = key_start + lax.broadcasted_iota(jnp.int32, shape, 0)
    allowed = (key_pos <= query_pos) & (key_ids == query_ids)
    return jnp.where(allowed, 0.0, MASKED)


def forward_kernel(
    first_block, heads, total, q_ref, k_ref, v_ref, ids_ref, row_info_ref, down_ref, *rest
):
    ctx_ref, lse_ref, rank_ref, q_out_ref, bias_ref = rest[-5:]
    block, step = pl.program_id(0), pl.program_id(1)
    rows = q_ref.shape[0]
    window = bias_ref.shape[0]
    row_start = (first_block + block) * rows
    start = jnp.clip(row_start - DOC_REACH, 0, total - window)
    start = pl.multiple_of(start, 16)

    @pl.when(step == 0)
    def _():
        bias_ref[...] = mask_bias(
            start,
            ids_ref[pl.ds(start, window), :],
            row_info_ref[0, 0:1, :],
            row_info_ref[0, 1:2, :],
            bias_ref.shape,
        )
        rank_ref[...] = jnp.zeros_like(rank_ref)

    queries = q_ref[...]
    q_out_ref[...] = queries
    stacked = stacked_heads(queries)
    keys = k_ref[pl.ds(start, window), :]
    values = v_ref[pl.ds(start, window), :]
    scores = dot_nt(keys, stacked) * (LOG2E / math.sqrt(HEAD_SIZE)) + bias_ref[...]
    top = jnp.max(scores, axis=0, keepdims=True)
    expanded = jnp.exp2(scores - top)
    total_weight = jnp.sum(expanded, axis=0, keepdims=True)
    probs = (expanded * (1.0 / total_weight)).astype(jnp.bfloat16)
    lse_ref[0, 0] = top + jnp.log(total_weight) * LOG2E
    context_t = dot_tn(values, probs)
    context = context_t.T.astype(jnp.bfloat16)
    for h in range(heads):
        part = context[h * rows : (h + 1) * rows]
        ctx_ref[:, h * HEAD_SIZE : (h + 1) * HEAD_SIZE] = part
        rank_ref[0] += dot_nt(down_ref[:, h * HEAD_SIZE : (h + 1) * HEAD_SIZE], part)


def backward_kernel(spec, scalars_ref, *refs):
    candidates, pieces, heads, group, total, first, final, with_up = spec
    refs = list(refs)

    def take(count):
        taken = refs[:count]
        del refs[:count]
        return taken

    sources = [take(pieces) for _ in range(candidates)]
    (w_ref, up_ref, down_ref, q_ref, ctx_ref, k_ref, v_ref, ids_ref, row_info_ref, lse_ref) = take(10)
    rank_ctx_ref = take(1)[0] if with_up else None
    if not first:
        _, dk_in, dv_in, dm_in = take(4)
    um_in = take(1)[0] if with_up else None
    dq_ref, dk_ref, dv_ref, dm_ref = take(4)
    um_ref = take(1)[0] if with_up else None
    x_ref, rank_ref, bias_ref, dk_sum, dv_sum, sems = take(6)
    if with_up:
        ctx_rank_ref = take(1)[0]

    step = pl.program_id(0)
    rows, width = x_ref.shape
    window = bias_ref.shape[0]
    tile = heads * HEAD_SIZE
    start = pl.multiple_of(scalars_ref[2], 16)
    gradient_scale = adapter_scale / math.sqrt(total)
    inv_scale = 1.0 / math.sqrt(HEAD_SIZE)

    @pl.when(step == 0)
    def _():
        for c, parts in enumerate(sources):

            @pl.when(scalars_ref[0] == c)
            def _(parts=parts):
                copies = []
                depth = rows // pieces
                for p, part in enumerate(parts):
                    copies.append(
                        pltpu.make_async_copy(
                            part, x_ref.at[pl.ds(p * depth, depth), :], sems.at[p]
                        )
                    )
                for copy in copies:
                    copy.start()
                for copy in copies:
                    copy.wait()

        bias_ref[...] = mask_bias(
            start,
            ids_ref[pl.ds(start, window), :],
            row_info_ref[0, 0:1, :],
            row_info_ref[0, 1:2, :],
            bias_ref.shape,
        )
        rank_ref[...] = three_parts(dot_nt(up_ref[...], x_ref[...]))
        if with_up:
            ctx_rank_ref[...] = three_parts(rank_ctx_ref[0])

    steps_per_kv = group // heads

    chunk = min(2048, width)

    def accumulate(i, acc):
        at = pl.multiple_of(i * chunk, chunk)
        return acc + dot_nt(x_ref[:, pl.ds(at, chunk)], w_ref[:, pl.ds(at, chunk)])

    down = down_ref[...]
    acc = adapter_scale * dot_tn(rank_ref[...], jnp.concatenate([down, down, down], axis=0))
    acc = lax.fori_loop(0, width // chunk, accumulate, acc)
    grad = acc.astype(jnp.bfloat16)

    queries = stacked_heads(q_ref[...])
    context = ctx_ref[...]
    grads = stacked_heads(grad)
    keys = k_ref[pl.ds(start, window), :]
    values = v_ref[pl.ds(start, window), :]
    delta = jnp.sum(
        (grads.astype(jnp.float32) * stacked_heads(context).astype(jnp.float32)).T,
        axis=0,
        keepdims=True,
    )
    scores = dot_nt(keys, queries) * (LOG2E * inv_scale) + bias_ref[...]
    probs = jnp.exp2(scores - lse_ref[0, 0])
    grad_probs = dot_nt(values, grads)
    grad_scores = (probs * (grad_probs - delta)).astype(jnp.bfloat16)
    probs_low = probs.astype(jnp.bfloat16)

    fresh = lax.rem(step, steps_per_kv) == 0

    @pl.when(fresh)
    def _():
        if first:
            dk_sum[...] = jnp.zeros_like(dk_sum)
            dv_sum[...] = jnp.zeros_like(dv_sum)
        else:
            dk_sum[...] = dk_in[...]
            dv_sum[...] = dv_in[...]

    dk_sum[pl.ds(start, window), :] += dot_nn(grad_scores, queries) * inv_scale
    dv_sum[pl.ds(start, window), :] += dot_nn(probs_low, grads)

    @pl.when(lax.rem(step, steps_per_kv) == steps_per_kv - 1)
    def _():
        dk_ref[...] = dk_sum[...].astype(dk_ref.dtype)
        dv_ref[...] = dv_sum[...].astype(dv_ref.dtype)

    grad_q = (dot_tn(keys, grad_scores) * inv_scale).T.astype(jnp.bfloat16)
    for h in range(heads):
        dq_ref[:, h * HEAD_SIZE : (h + 1) * HEAD_SIZE] = grad_q[h * rows : (h + 1) * rows]

    down_part = gradient_scale * folded(dot_nn(rank_ref[...], context))
    dm_ref[...] = down_part if first else dm_in[...] + down_part
    if with_up:
        at = pl.multiple_of(scalars_ref[3] + step * tile, tile)
        um_ref[...] = um_in[...] + gradient_scale * folded(
            dot_nn(ctx_rank_ref[...], x_ref[:, pl.ds(at, tile)])
        )


def per_device(
    handoff_gradient,
    output_weight,
    adapter_down,
    adapter_up,
    stored_queries,
    stored_keys,
    stored_values,
    segments,
):
    pipe_count = lax.axis_size("pipe")
    line = lax.axis_size("fsdp")
    member = lax.axis_index("fsdp")
    shard = handoff_gradient.shape[1]
    total = shard * line
    model_width = handoff_gradient.shape[2]
    query_width = stored_queries.shape[2]
    kv_width = stored_keys.shape[2]
    rank = adapter_down.shape[1]
    query_heads = query_width // HEAD_SIZE
    kv_heads = kv_width // HEAD_SIZE
    group = query_heads // kv_heads
    local_width = adapter_up.shape[2]
    bf16, f32 = jnp.bfloat16, jnp.float32

    split = 2
    depth = shard // split
    from_next = [((i + 1) % pipe_count, i) for i in range(pipe_count)]
    mirrored = [(i, pipe_count - 1 - i) for i in range(pipe_count)]
    own = [
        lax.ppermute(handoff_gradient[0, p * depth : (p + 1) * depth], "pipe", from_next)
        for p in range(split)
    ]
    rising, falling = [own], [own]
    for k in range(1, line):
        up_pairs = [(i, i + 1) for i in range(k - 1, line - 1)]
        down_pairs = [(i + 1, i) for i in range(line - k)]
        up_now, down_now = [], []
        for p in range(split):
            up_now.append(lax.ppermute(rising[-1][p], "fsdp", up_pairs))
            down_now.append(lax.ppermute(falling[-1][p], "fsdp", down_pairs))
        rising.append(up_now)
        falling.append(down_now)

    up_full = lax.all_gather(adapter_up[0], "fsdp", axis=1, tiled=True)
    key_local = lax.ppermute(stored_keys[0], "pipe", mirrored)
    value_local = lax.ppermute(stored_values[0], "pipe", mirrored)
    query_half = [
        lax.ppermute(stored_queries[0, i * (total // 2) : (i + 1) * (total // 2)], "pipe", mirrored)
        for i in range(2)
    ]

    ids_column = segments[0][:, None]
    rows_f = total // 4
    heads_f = 2
    steps_f = query_heads // heads_f
    lanes_f = heads_f * rows_f
    window_f = min(total, rows_f + DOC_REACH)
    down = adapter_down[0]

    def row_info(rows, heads):
        pos = jnp.arange(total, dtype=jnp.int32).reshape(total // rows, 1, rows)
        ids = segments[0].reshape(total // rows, 1, rows)
        both = jnp.concatenate([pos, ids], axis=1)
        return jnp.tile(both, (1, 1, heads))

    forward_out = None
    info_f = row_info(rows_f, heads_f)
    for i in range(2):
        base = 2 * i
        in_specs = [
            pl.BlockSpec((rows_f, heads_f * HEAD_SIZE), lambda b, n: (b, n)),
            pl.BlockSpec((total, HEAD_SIZE), lambda b, n: (0, n * heads_f // group)),
            pl.BlockSpec((total, HEAD_SIZE), lambda b, n: (0, n * heads_f // group)),
            pl.BlockSpec((total, 1), lambda b, n: (0, 0)),
            pl.BlockSpec((1, 2, lanes_f), lambda b, n, base=base: (base + b, 0, 0)),
            pl.BlockSpec((rank, heads_f * HEAD_SIZE), lambda b, n: (0, n)),
        ]
        operands = [query_half[i], key_local, value_local, ids_column, info_f, down]
        aliases = {}
        if forward_out is not None:
            for j, a in enumerate(forward_out):
                aliases[len(operands)] = j
                operands.append(a)
                in_specs.append(pl.BlockSpec(memory_space=pl.ANY))
        forward_out = pl.pallas_call(
            functools.partial(forward_kernel, base, heads_f, total),
            grid=(2, steps_f),
            in_specs=in_specs,
            out_specs=[
                pl.BlockSpec((rows_f, heads_f * HEAD_SIZE), lambda b, n, base=base: (base + b, n)),
                pl.BlockSpec((1, 1, 1, lanes_f), lambda b, n, base=base: (base + b, n, 0, 0)),
                pl.BlockSpec((1, rank, rows_f), lambda b, n, base=base: (base + b, 0, 0)),
                pl.BlockSpec((rows_f, heads_f * HEAD_SIZE), lambda b, n, base=base: (base + b, n)),
            ],
            out_shape=[
                jax.ShapeDtypeStruct((total, query_width), bf16),
                jax.ShapeDtypeStruct((4, steps_f, 1, lanes_f), f32),
                jax.ShapeDtypeStruct((4, rank, rows_f), f32),
                jax.ShapeDtypeStruct((total, query_width), bf16),
            ],
            scratch_shapes=[pltpu.VMEM((window_f, lanes_f), f32)],
            input_output_aliases=aliases,
            compiler_params=pltpu.CompilerParams(
                dimension_semantics=("arbitrary", "arbitrary"), vmem_limit_bytes=VMEM_BYTES
            ),
            cost_estimate=pl.CostEstimate(
                flops=2 * 2 * total // 2 * window_f * query_width,
                bytes_accessed=4 * total * query_width,
                transcendentals=total // 2 * window_f * query_heads,
            ),
            name=f"forward_{i}",
        )(*operands)
    context, lse, rank_portion, query = forward_out
    rank_context = jnp.sum(lax.all_gather(rank_portion, "fsdp", axis=0), axis=0)

    def by_rows(rows, heads):
        normal = (
            lse.reshape(4, query_heads, rows_f // rows, rows)
            .transpose(0, 2, 1, 3)
            .reshape(total // rows, query_heads // heads, 1, heads * rows)
        )
        ranks = (
            rank_context.reshape(4, rank, rows_f // rows, rows)
            .transpose(0, 2, 1, 3)
            .reshape(total // rows, rank, rows)
        )
        return normal, ranks, row_info(rows, heads)

    tables = {}

    def backward(sources, choice, row_block, rows, state, up_map, final, name):
        first = state is None
        with_up = up_map is not None
        heads = max(1, min(group, 4, 384 // rows))
        if (rows, heads) not in tables:
            tables[rows, heads] = by_rows(rows, heads)
        normal, ranks, info = tables[rows, heads]
        tile = heads * HEAD_SIZE
        steps = query_heads // heads
        lanes = heads * rows
        window = min(total, rows + DOC_REACH)
        pieces = len(sources[0])
        start = jnp.clip(row_block * rows - DOC_REACH, 0, total - window)
        scalars = jnp.stack([choice, row_block, start, member * local_width]).astype(jnp.int32)
        anywhere = pl.BlockSpec(memory_space=pl.ANY)
        per_kv = group // heads
        kv_spec = pl.BlockSpec((total, HEAD_SIZE), lambda n, s: (0, n // per_kv))
        row_spec = pl.BlockSpec((rows, tile), lambda n, s: (s[1], n))
        rank_spec = pl.BlockSpec((rank, tile), lambda n, s: (0, n))
        operands = [part for parts in sources for part in parts]
        in_specs = [anywhere] * len(operands)
        operands += [
            output_weight[0],
            up_full,
            down,
            query,
            context,
            key_local,
            value_local,
            ids_column,
            info,
            normal,
        ]
        in_specs += [
            pl.BlockSpec((tile, model_width), lambda n, s: (n, 0)),
            pl.BlockSpec((rank, model_width), lambda n, s: (0, 0)),
            rank_spec,
            row_spec,
            row_spec,
            kv_spec,
            kv_spec,
            pl.BlockSpec((total, 1), lambda n, s: (0, 0)),
            pl.BlockSpec((1, 2, lanes), lambda n, s: (s[1], 0, 0)),
            pl.BlockSpec((1, 1, 1, lanes), lambda n, s: (s[1], n, 0, 0)),
        ]
        if with_up:
            operands.append(ranks)
            in_specs.append(pl.BlockSpec((1, rank, rows), lambda n, s: (s[1], 0, 0)))
        aliases = {}
        if not first:
            aliases[1 + len(operands)] = 0
            if not final:
                aliases[2 + len(operands)] = 1
                aliases[3 + len(operands)] = 2
            operands += list(state)
            in_specs += [anywhere, kv_spec, kv_spec, rank_spec]
        if with_up:
            operands.append(up_map)
            in_specs.append(rank_spec)
        kv_type = bf16 if final else f32
        out_shape = [
            jax.ShapeDtypeStruct((total, query_width), bf16),
            jax.ShapeDtypeStruct((total, kv_width), kv_type),
            jax.ShapeDtypeStruct((total, kv_width), kv_type),
            jax.ShapeDtypeStruct((rank, query_width), f32),
        ]
        out_specs = [row_spec, kv_spec, kv_spec, rank_spec]
        scratch = [
            pltpu.VMEM((rows, model_width), bf16),
            pltpu.VMEM((3 * rank, rows), bf16),
            pltpu.VMEM((window, lanes), f32),
            pltpu.VMEM((total, HEAD_SIZE), f32),
            pltpu.VMEM((total, HEAD_SIZE), f32),
            pltpu.SemaphoreType.DMA((pieces,)),
        ]
        if with_up:
            out_shape.append(jax.ShapeDtypeStruct((rank, query_width), f32))
            out_specs.append(rank_spec)
            scratch.append(pltpu.VMEM((3 * rank, rows), bf16))
        out = pl.pallas_call(
            functools.partial(
                backward_kernel, (len(sources), pieces, heads, group, total, first, final, with_up)
            ),
            grid_spec=pltpu.PrefetchScalarGridSpec(
                num_scalar_prefetch=1,
                grid=(steps,),
                in_specs=in_specs,
                out_specs=out_specs,
                scratch_shapes=scratch,
            ),
            out_shape=out_shape,
            input_output_aliases=aliases,
            compiler_params=pltpu.CompilerParams(
                dimension_semantics=("arbitrary",), vmem_limit_bytes=VMEM_BYTES
            ),
            cost_estimate=pl.CostEstimate(
                flops=2 * rows * model_width * query_width + 10 * rows * window * query_width,
                bytes_accessed=2 * model_width * query_width,
                transcendentals=rows * window * query_heads,
            ),
            name=name,
        )(scalars, *operands)
        return tuple(out[:4]), (out[4] if with_up else None)

    def arrival(device, order):
        found = []
        for k in range(1, line):
            if device >= k:
                found.append((k, True, device - k))
            if device + k < line:
                found.append((k, False, device + k))
        return found[order]

    def table_at(values):
        return jnp.asarray(values, jnp.int32)[member]

    zero = jnp.int32(0)
    state, _ = backward([own], zero, member, shard, None, None, False, "own")
    scale = adapter_scale / math.sqrt(total)

    def chosen(order):
        entries = [arrival(d, order) for d in range(line)]
        kinds = sorted({(k, rises) for k, rises, _ in entries})
        choice = table_at([kinds.index((k, rises)) for k, rises, _ in entries])
        owner = table_at([o for _, _, o in entries])
        sources = [(rising if rises else falling)[k] for k, rises in kinds]
        return sources, choice, owner

    ranks_whole = rank_context.reshape(4, rank, rows_f).transpose(1, 0, 2).reshape(rank, total)

    own_columns = jnp.concatenate(
        [lax.dynamic_slice_in_dim(part, member * local_width, local_width, 1) for part in own], axis=0
    )
    own_ranks = lax.dynamic_slice_in_dim(ranks_whole, member * shard, shard, 1)
    up_map = scale * jnp.dot(own_ranks, own_columns.astype(f32), precision=lax.Precision.HIGHEST)
    for order in range(line - 1):
        sources, choice, owner = chosen(order)
        if order < line - 2:
            state, up_map = backward(
                sources, choice, owner, shard, state, up_map, False, f"arrived_{order}"
            )
        else:
            for p in range(split):
                state, up_map = backward(
                    [[s[p]] for s in sources],
                    choice,
                    owner * split + p,
                    depth,
                    state,
                    up_map,
                    p == split - 1,
                    f"arrived_{order}_{p}",
                )
    query_gradient, key_gradient, value_gradient, down_map = state
    return (
        query_gradient[None],
        key_gradient[None],
        value_gradient[None],
        down_map[None],
        up_map[None],
    )


def solution(mesh):
    placed = (
        P("pipe", "fsdp", None),
        P("pipe", "fsdp", None),
        P("pipe", None, "fsdp"),
        P("pipe", None, "fsdp"),
        P("pipe", None, "fsdp"),
        P("pipe", None, "fsdp"),
        P("pipe", None, "fsdp"),
        P("pipe", None),
    )
    return jax.shard_map(
        per_device,
        mesh=mesh,
        in_specs=placed,
        out_specs=(
            P("pipe", None, "fsdp"),
            P("pipe", None, "fsdp"),
            P("pipe", None, "fsdp"),
            P("pipe", None, "fsdp"),
            P("pipe", None, "fsdp"),
        ),
        check_vma=False,
    )
```

```python
import functools
import math

import jax
import jax.numpy as jnp
import numpy as np
from jax import lax
from jax.experimental import pallas as pl
from jax.experimental.pallas import tpu as pltpu
from jax.sharding import PartitionSpec as P

HEAD_SIZE = 128
DOC_REACH = 384
MASKED = -1e30
LOG2E = math.log2(math.e)
VMEM_BYTES = 40 * 2**20
FLOPS_PER_MICRO = 1.0e9

adapter_scale = 2.0


def dot_nt(a, b):
    return lax.dot_general(a, b, (((1,), (1,)), ((), ())), preferred_element_type=jnp.float32)


def dot_nn(a, b):
    return lax.dot_general(a, b, (((1,), (0,)), ((), ())), preferred_element_type=jnp.float32)


def dot_tn(a, b):
    return lax.dot_general(a, b, (((0,), (0,)), ((), ())), preferred_element_type=jnp.float32)


def three_parts(a):
    high = a.astype(jnp.bfloat16)
    rest = a - high.astype(jnp.float32)
    middle = rest.astype(jnp.bfloat16)
    low = (rest - middle.astype(jnp.float32)).astype(jnp.bfloat16)
    return jnp.concatenate([high, middle, low], axis=0)


def folded(a):
    rows = a.shape[0] // 3
    return a[:rows] + a[rows : 2 * rows] + a[2 * rows :]


def stacked_heads(a):
    count = a.shape[1] // HEAD_SIZE
    return jnp.concatenate(
        [a[:, h * HEAD_SIZE : (h + 1) * HEAD_SIZE] for h in range(count)], axis=0
    )


def mask_bias(key_start, key_ids, query_pos, query_ids, shape):
    key_pos = key_start + lax.broadcasted_iota(jnp.int32, shape, 0)
    allowed = (key_pos <= query_pos) & (key_ids == query_ids)
    return jnp.where(allowed, 0.0, MASKED)


def forward_kernel(
    first_block, heads, total, q_ref, k_ref, v_ref, ids_ref, row_info_ref, down_ref, *rest
):
    ctx_ref, lse_ref, rank_ref, q_out_ref, bias_ref = rest[-5:]
    block, step = pl.program_id(0), pl.program_id(1)
    rows = q_ref.shape[0]
    window = bias_ref.shape[0]
    row_start = (first_block + block) * rows
    start = jnp.clip(row_start - DOC_REACH, 0, total - window)
    start = pl.multiple_of(start, 16)

    @pl.when(step == 0)
    def _():
        bias_ref[...] = mask_bias(
            start,
            ids_ref[pl.ds(start, window), :],
            row_info_ref[0, 0:1, :],
            row_info_ref[0, 1:2, :],
            bias_ref.shape,
        )
        rank_ref[...] = jnp.zeros_like(rank_ref)

    queries = q_ref[...]
    q_out_ref[...] = queries
    stacked = stacked_heads(queries)
    keys = k_ref[pl.ds(start, window), :]
    values = v_ref[pl.ds(start, window), :]
    scores = dot_nt(keys, stacked) * (LOG2E / math.sqrt(HEAD_SIZE)) + bias_ref[...]
    top = jnp.max(scores, axis=0, keepdims=True)
    expanded = jnp.exp2(scores - top)
    total_weight = jnp.sum(expanded, axis=0, keepdims=True)
    probs = (expanded * (1.0 / total_weight)).astype(jnp.bfloat16)
    lse_ref[0, 0] = top + jnp.log(total_weight) * LOG2E
    context_t = dot_tn(values, probs)
    context = context_t.T.astype(jnp.bfloat16)
    for h in range(heads):
        part = context[h * rows : (h + 1) * rows]
        ctx_ref[:, h * HEAD_SIZE : (h + 1) * HEAD_SIZE] = part
        rank_ref[0] += dot_nt(down_ref[:, h * HEAD_SIZE : (h + 1) * HEAD_SIZE], part)


def fetch(choice, groups, x_ref, sems):
    for c, parts in enumerate(groups):

        @pl.when(choice == c)
        def _(parts=parts):
            copies = []
            at = 0
            for p, part in enumerate(parts):
                width = part.shape[1]
                copies.append(
                    pltpu.make_async_copy(part, x_ref.at[:, pl.ds(at, width)], sems.at[p])
                )
                at += width
            for copy in copies:
                copy.start()
            for copy in copies:
                copy.wait()


def rank_product(up_ref, x_ref, first_column):
    local = up_ref.shape[2]
    width = x_ref.shape[1]
    total = None
    for j in range(width // local):
        part = dot_nt(up_ref[first_column // local + j], x_ref[:, j * local : (j + 1) * local])
        total = part if total is None else total + part
    return total


def project(x_ref, w_ref, acc):
    width = x_ref.shape[1]
    for at in range(0, width, 4096):
        to = min(at + 4096, width)
        acc = acc + dot_nt(x_ref[:, at:to], w_ref[:, at:to])
    return acc


def rank_term(rank, down):
    return adapter_scale * dot_tn(rank, jnp.concatenate([down, down, down], axis=0))


def projection_kernel(spec, scalars_ref, *refs):
    at_choice, candidates, pieces, before, ends, after = spec
    refs = list(refs)

    def take(count):
        taken = refs[:count]
        del refs[:count]
        return taken

    groups = [take(pieces) for _ in range(candidates)]
    first_column = sum(part.shape[1] for part in groups[0][:before])
    w_ref, up_ref, down_ref = take(3)
    if before:
        acc_in, rank_in = take(2)
    take(after)
    out_ref, rank_out = take(2)
    if ends:
        local_out = take(1)[0]
    x_ref, sems = take(2)
    if ends:
        parts_ref, local_ref = take(2)
    step = pl.program_id(0)

    @pl.when(step == 0)
    def _():
        fetch(scalars_ref[at_choice], [parts[before:] for parts in groups], x_ref, sems)
        rank = rank_product(up_ref, x_ref, first_column)
        rank_out[...] = rank + rank_in[...] if before else rank
        if ends:
            parts_ref[...] = three_parts(rank_out[...])
            for c, parts in enumerate(groups):
                at = 0
                for part in parts:
                    width = part.shape[1]
                    mine = scalars_ref[0] - at

                    @pl.when((scalars_ref[at_choice] == c) & (mine >= 0) & (mine < width))
                    def _(part=part, mine=mine):
                        copy = pltpu.make_async_copy(
                            part.at[:, pl.ds(pl.multiple_of(mine, 128), local_ref.shape[1])],
                            local_ref,
                            sems.at[0],
                        )
                        copy.start()
                        copy.wait()

                    at += width

    if ends:
        begin = rank_term(parts_ref[...], down_ref[...])
        if before:
            begin = begin + acc_in[...]
    else:
        begin = acc_in[...] if before else jnp.zeros(out_ref.shape, jnp.float32)
    out_ref[...] = project(x_ref, w_ref, begin).astype(out_ref.dtype)
    if ends:
        tile = local_out.shape[1]
        local_out[...] = local_ref[:, pl.ds(pl.multiple_of(step * tile, tile), tile)]


def up_map_kernel(count, scalars_ref, *refs):
    ranks = refs[:count]
    columns = refs[count : 2 * count]
    out_ref = refs[2 * count]
    rows_total = sum(c.shape[0] for c in columns)
    scale = adapter_scale / math.sqrt(rows_total * (count + 1) // count)
    total = None
    for rank, column in zip(ranks, columns):
        part = folded(dot_nn(three_parts(rank[0]), column[...]))
        total = part if total is None else total + part
    out_ref[...] = scale * total


def attention_backward(
    heads, steps_per_kv, step, start, inv_scale, grad, q_ref, ctx_ref, k_ref, v_ref, lse_ref,
    bias_ref, dk_sum, dv_sum, fresh_sums, dq_ref,
):
    window = bias_ref.shape[0]
    rows = grad.shape[0]
    queries = stacked_heads(q_ref[...])
    grads = stacked_heads(grad)
    keys = k_ref[pl.ds(start, window), :]
    values = v_ref[pl.ds(start, window), :]
    delta = jnp.sum(
        (grads.astype(jnp.float32) * stacked_heads(ctx_ref[...]).astype(jnp.float32)).T,
        axis=0,
        keepdims=True,
    )
    scores = dot_nt(keys, queries) * (LOG2E * inv_scale) + bias_ref[...]
    probs = jnp.exp2(scores - lse_ref[0, 0])
    grad_probs = dot_nt(values, grads)
    grad_scores = (probs * (grad_probs - delta)).astype(jnp.bfloat16)
    probs_low = probs.astype(jnp.bfloat16)

    @pl.when(lax.rem(step, steps_per_kv) == 0)
    def _():
        fresh_sums()

    dk_sum[pl.ds(start, window), :] += dot_nn(grad_scores, queries) * inv_scale
    dv_sum[pl.ds(start, window), :] += dot_nn(probs_low, grads)
    grad_q = (dot_tn(keys, grad_scores) * inv_scale).T.astype(jnp.bfloat16)
    for h in range(heads):
        dq_ref[:, h * HEAD_SIZE : (h + 1) * HEAD_SIZE] = grad_q[h * rows : (h + 1) * rows]


def backward_kernel(spec, scalars_ref, *refs):
    here, heads, group, total, first, last, after = spec
    refs = list(refs)

    def take(count):
        taken = refs[:count]
        del refs[:count]
        return taken

    if last:
        local_ref, rank_ctx_ref, um_in = take(3)
    grad_ref, rank_in, q_ref, ctx_ref, k_ref, v_ref, ids_ref, row_info_ref, lse_ref = take(9)
    if not first:
        _, dk_in, dv_in, dm_in = take(4)
    take(after)
    dq_ref, dk_ref, dv_ref, dm_ref = take(4)
    if last:
        um_ref = take(1)[0]
    bias_ref, parts_ref, dk_sum, dv_sum = take(4)

    step = pl.program_id(0)
    window = bias_ref.shape[0]
    start = pl.multiple_of(scalars_ref[here + 1], 16)
    gradient_scale = adapter_scale / math.sqrt(total)
    inv_scale = 1.0 / math.sqrt(HEAD_SIZE)
    steps_per_kv = group // heads

    @pl.when(step == 0)
    def _():
        parts_ref[...] = three_parts(rank_in[...])
        bias_ref[...] = mask_bias(
            start,
            ids_ref[pl.ds(start, window), :],
            row_info_ref[0, 0:1, :],
            row_info_ref[0, 1:2, :],
            bias_ref.shape,
        )

    def fresh_sums():
        if first:
            dk_sum[...] = jnp.zeros_like(dk_sum)
            dv_sum[...] = jnp.zeros_like(dv_sum)
        else:
            dk_sum[...] = dk_in[...]
            dv_sum[...] = dv_in[...]

    attention_backward(
        heads, steps_per_kv, step, start, inv_scale, grad_ref[...], q_ref, ctx_ref, k_ref, v_ref,
        lse_ref, bias_ref, dk_sum, dv_sum, fresh_sums, dq_ref,
    )

    @pl.when(lax.rem(step, steps_per_kv) == steps_per_kv - 1)
    def _():
        dk_ref[...] = dk_sum[...].astype(dk_ref.dtype)
        dv_ref[...] = dv_sum[...].astype(dv_ref.dtype)

    down_part = gradient_scale * folded(dot_nn(parts_ref[...], ctx_ref[...]))
    dm_ref[...] = down_part if first else dm_in[...] + down_part
    if last:
        um_ref[...] = um_in[...] + gradient_scale * folded(
            dot_nn(three_parts(rank_ctx_ref[0]), local_ref[...])
        )


def options(name, micros):
    return dict(
        compiler_params=pltpu.CompilerParams(
            dimension_semantics=("arbitrary",), vmem_limit_bytes=VMEM_BYTES
        ),
        cost_estimate=pl.CostEstimate(
            flops=int(micros * FLOPS_PER_MICRO), bytes_accessed=1, transcendentals=0
        ),
        name=name,
    )


ANYWHERE = pl.BlockSpec(memory_space=pl.ANY)


def per_device(
    handoff_gradient,
    output_weight,
    adapter_down,
    adapter_up,
    stored_queries,
    stored_keys,
    stored_values,
    segments,
):
    pipe_count = lax.axis_size("pipe")
    line = lax.axis_size("fsdp")
    member = lax.axis_index("fsdp")
    shard = handoff_gradient.shape[1]
    total = shard * line
    model_width = handoff_gradient.shape[2]
    query_width = stored_queries.shape[2]
    kv_width = stored_keys.shape[2]
    rank = adapter_down.shape[1]
    query_heads = query_width // HEAD_SIZE
    kv_heads = kv_width // HEAD_SIZE
    group = query_heads // kv_heads
    local_width = adapter_up.shape[2]
    bf16, f32 = jnp.bfloat16, jnp.float32
    weight = output_weight[0]
    down = adapter_down[0]

    def spread(block):
        blocks = [block]
        for d in range(1, line):
            route = [(i, (i + d) % line) for i in range(line)]
            blocks.append(lax.ppermute(block, "fsdp", route))
        turned = jnp.stack(blocks[::-1] + blocks[::-1])
        return lax.dynamic_slice_in_dim(turned, line - 1 - member, line, 0)

    from_next = [((i + 1) % pipe_count, i) for i in range(pipe_count)]
    mirrored = [(i, pipe_count - 1 - i) for i in range(pipe_count)]
    widths = [model_width // 4, model_width // 2, model_width // 4]
    pieces = len(widths)
    own, at = [], 0
    for width in widths:
        part = handoff_gradient[0, :, at : at + width]
        if own:
            part, _ = lax.optimization_barrier((part, own[-1]))
        own.append(lax.ppermute(part, "pipe", from_next))
        at += width
    up_all = spread(lax.optimization_barrier((adapter_up[0], own[0]))[0])
    rising, falling = [own], [own]

    def pass_on(tokens):
        k = len(rising)
        if k >= line:
            return
        up_pairs = [(i, i + 1) for i in range(k - 1, line - 1)]
        down_pairs = [(i + 1, i) for i in range(line - k)]
        up_now, down_now = [], []
        for p in range(pieces):
            up_part, down_part = rising[-1][p], falling[-1][p]
            if tokens is not None:
                up_part, down_part, _ = lax.optimization_barrier((up_part, down_part, tokens[p]))
            up_now.append(lax.ppermute(up_part, "fsdp", up_pairs))
            down_now.append(lax.ppermute(down_part, "fsdp", down_pairs))
        rising.append(up_now)
        falling.append(down_now)

    pass_on(None)
    saved_k, saved_v, saved_q, _ = lax.optimization_barrier(
        (stored_keys[0], stored_values[0], stored_queries[0], own[1])
    )
    key_local = lax.ppermute(saved_k, "pipe", mirrored)
    value_local = lax.ppermute(saved_v, "pipe", mirrored)
    half = total // 2
    query_half = [
        lax.ppermute(saved_q[i * half : (i + 1) * half], "pipe", mirrored) for i in range(2)
    ]

    def arrival(device, order):
        found = []
        for k in range(1, line):
            if device >= k:
                found.append((k, True, device - k))
            if device + k < line:
                found.append((k, False, device + k))
        return found[order]

    def groups_of(order):
        if order < 0:
            return [(0, True)]
        return sorted({arrival(d, order)[:2] for d in range(line)})

    def choices(order):
        return [(rising if rises else falling)[k] for k, rises in groups_of(order)]

    window = min(total, shard + DOC_REACH)
    table = np.zeros((line, 1 + 3 * line), np.int32)
    for d in range(line):
        table[d, 0] = d * local_width
        for order in range(-1, line - 1):
            found = (0, True, d) if order < 0 else arrival(d, order)
            first_key = min(max(found[2] * shard - DOC_REACH, 0), total - window)
            at = 4 + 3 * order
            table[d, at : at + 3] = groups_of(order).index(found[:2]), found[2], first_key
    scalars = lax.dynamic_index_in_dim(jnp.asarray(table), member, 0, keepdims=False)

    tile_p = min(512, query_width)

    def projection(order, after, low=0, high=pieces, sums=()):
        groups = choices(order)
        ends = high == pieces
        groups = [parts[:high] for parts in groups]
        width = sum(widths[low:high])
        block, odd = divmod(sum(widths[:low]), width)
        assert odd == 0
        operands = [part for parts in groups for part in parts]
        in_specs = [ANYWHERE] * len(operands)
        rank_spec = pl.BlockSpec((rank, shard), lambda n, s: (0, 0))
        tile_spec = pl.BlockSpec((shard, tile_p), lambda n, s: (0, n))
        operands += [weight, up_all, down, *sums, *after]
        in_specs += [
            pl.BlockSpec((tile_p, width), lambda n, s: (n, block)),
            pl.BlockSpec((line, rank, local_width), lambda n, s: (0, 0, 0)),
            pl.BlockSpec((rank, tile_p), lambda n, s: (0, n)),
        ]
        in_specs += [tile_spec, rank_spec][: len(sums)] + [ANYWHERE] * len(after)
        out_shape = [
            jax.ShapeDtypeStruct((shard, query_width), bf16 if ends else f32),
            jax.ShapeDtypeStruct((rank, shard), f32),
        ]
        out_specs = [tile_spec, rank_spec]
        scratch = [
            pltpu.VMEM((shard, width), bf16),
            pltpu.SemaphoreType.DMA((high - low,)),
        ]
        if ends:
            out_shape.append(jax.ShapeDtypeStruct((shard, local_width), bf16))
            out_specs.append(
                pl.BlockSpec((shard, local_width * tile_p // query_width), lambda n, s: (0, n))
            )
            scratch.append(pltpu.VMEM((3 * rank, shard), bf16))
            scratch.append(pltpu.VMEM((shard, local_width), bf16))
        return pl.pallas_call(
            functools.partial(
                projection_kernel, (4 + 3 * order, len(groups), high, low, ends, len(after))
            ),
            grid_spec=pltpu.PrefetchScalarGridSpec(
                num_scalar_prefetch=1,
                grid=(query_width // tile_p,),
                in_specs=in_specs,
                out_specs=out_specs,
                scratch_shapes=scratch,
            ),
            out_shape=out_shape,
            **options(f"projection_{order + 1}_{high}", 20 * (high - low) / pieces),
        )(scalars, *operands)

    projected = [projection(-1, [])]
    done_before = projected[0][1]
    if line > 2:
        pass_on([done_before] * pieces)
        projected.append(projection(0, [done_before, key_local, value_local, query_half[0]]))
        done_before = projected[1][1]

    ids_column = segments[0][:, None]
    rows_f = total // 4
    heads_f = 2
    steps_f = query_heads // heads_f
    lanes_f = heads_f * rows_f
    window_f = min(total, rows_f + DOC_REACH)

    def row_info(rows, heads):
        pos = jnp.arange(total, dtype=jnp.int32).reshape(total // rows, 1, rows)
        ids = segments[0].reshape(total // rows, 1, rows)
        both = jnp.concatenate([pos, ids], axis=1)
        return jnp.tile(both, (1, 1, heads))

    def waits(piece):
        return [rising[2][piece], falling[2][piece]] if line > 2 else []

    forward_out = None
    normalisers = []
    info_f = row_info(rows_f, heads_f)
    for i in range(2):
        base = 2 * i
        in_specs = [
            pl.BlockSpec((rows_f, heads_f * HEAD_SIZE), lambda b, n: (b, n)),
            pl.BlockSpec((total, HEAD_SIZE), lambda b, n: (0, n * heads_f // group)),
            pl.BlockSpec((total, HEAD_SIZE), lambda b, n: (0, n * heads_f // group)),
            pl.BlockSpec((total, 1), lambda b, n: (0, 0)),
            pl.BlockSpec((1, 2, lanes_f), lambda b, n, base=base: (base + b, 0, 0)),
            pl.BlockSpec((rank, heads_f * HEAD_SIZE), lambda b, n: (0, n)),
        ]
        operands = [query_half[i], key_local, value_local, ids_column, info_f, down]
        aliases = {}
        if forward_out is None:
            pins = [done_before] + waits(0)
            operands += pins
            in_specs += [ANYWHERE] * len(pins)
        else:
            for j, a in enumerate(forward_out):
                aliases[len(operands)] = j
                operands.append(a)
                in_specs.append(ANYWHERE)
            operands += waits(1)
            in_specs += [ANYWHERE] * len(waits(1))
        settings = options(f"forward_{i}", 18)
        settings["compiler_params"] = pltpu.CompilerParams(
            dimension_semantics=("arbitrary", "arbitrary"), vmem_limit_bytes=VMEM_BYTES
        )
        forward_out = pl.pallas_call(
            functools.partial(forward_kernel, base, heads_f, total),
            grid=(2, steps_f),
            in_specs=in_specs,
            out_specs=[
                pl.BlockSpec((rows_f, heads_f * HEAD_SIZE), lambda b, n, base=base: (base + b, n)),
                pl.BlockSpec((1, 1, 1, lanes_f), lambda b, n, base=base: (base + b, n, 0, 0)),
                pl.BlockSpec((1, rank, rows_f), lambda b, n, base=base: (base + b, 0, 0)),
                pl.BlockSpec((rows_f, heads_f * HEAD_SIZE), lambda b, n, base=base: (base + b, n)),
            ],
            out_shape=[
                jax.ShapeDtypeStruct((total, query_width), bf16),
                jax.ShapeDtypeStruct((4, steps_f, 1, lanes_f), f32),
                jax.ShapeDtypeStruct((4, rank, rows_f), f32),
                jax.ShapeDtypeStruct((total, query_width), bf16),
            ],
            scratch_shapes=[pltpu.VMEM((window_f, lanes_f), f32)],
            input_output_aliases=aliases,
            **settings,
        )(*operands)
        normalisers.append(forward_out[1])
    context, lse, rank_portion, query = forward_out

    rank_context = rank_portion
    for d in range(1, line):
        route = [(i, (i + d) % line) for i in range(line)]
        rank_context = rank_context + lax.ppermute(rank_portion, "fsdp", route)

    rows = shard
    heads = max(1, min(group, 384 // rows))
    normal = (
        lse.reshape(4, query_heads, rows_f // rows, rows)
        .transpose(0, 2, 1, 3)
        .reshape(total // rows, query_heads // heads, 1, heads * rows)
    )
    ranks = (
        rank_context.reshape(4, rank, rows_f // rows, rows)
        .transpose(0, 2, 1, 3)
        .reshape(total // rows, rank, rows)
    )
    info = row_info(rows, heads)
    tile = heads * HEAD_SIZE
    lanes = heads * rows
    per_kv = group // heads
    kv_spec = pl.BlockSpec((total, HEAD_SIZE), lambda n, s: (0, n // per_kv))
    tile_spec = pl.BlockSpec((rows, tile), lambda n, s: (0, n))
    map_spec = pl.BlockSpec((rank, tile), lambda n, s: (0, n))
    rank_spec = pl.BlockSpec((rank, rows), lambda n, s: (0, 0))

    def backward(order, state, source, up_map=None, after=()):
        first = state is None
        last = up_map is not None
        here = 5 + 3 * order
        row_spec = pl.BlockSpec((rows, tile), lambda n, s: (s[here], n))
        ctx_rank_spec = pl.BlockSpec((1, rank, rows), lambda n, s: (s[here], 0, 0))
        operands, in_specs = [], []
        grad, rank_grad, local_columns = source
        if last:
            operands += [local_columns, ranks, up_map]
            in_specs += [tile_spec, ctx_rank_spec, map_spec]
        operands += [
            grad,
            rank_grad,
            query,
            context,
            key_local,
            value_local,
            ids_column,
            info,
            normal,
        ]
        in_specs += [
            tile_spec,
            rank_spec,
            row_spec,
            row_spec,
            kv_spec,
            kv_spec,
            pl.BlockSpec((total, 1), lambda n, s: (0, 0)),
            pl.BlockSpec((1, 2, lanes), lambda n, s: (s[here], 0, 0)),
            pl.BlockSpec((1, 1, 1, lanes), lambda n, s: (s[here], n, 0, 0)),
        ]
        aliases = {}
        if not first:
            aliases[1 + len(operands)] = 0
            operands += list(state)
            in_specs += [ANYWHERE, kv_spec, kv_spec, map_spec]
        operands += list(after)
        in_specs += [ANYWHERE] * len(after)
        kv_type = bf16 if last else f32
        out_shape = [
            jax.ShapeDtypeStruct((total, query_width), bf16),
            jax.ShapeDtypeStruct((total, kv_width), kv_type),
            jax.ShapeDtypeStruct((total, kv_width), kv_type),
            jax.ShapeDtypeStruct((rank, query_width), f32),
        ]
        out_specs = [row_spec, kv_spec, kv_spec, map_spec]
        scratch = [
            pltpu.VMEM((window, lanes), f32),
            pltpu.VMEM((3 * rank, rows), bf16),
            pltpu.VMEM((total, HEAD_SIZE), f32),
            pltpu.VMEM((total, HEAD_SIZE), f32),
        ]
        if last:
            out_shape.append(jax.ShapeDtypeStruct((rank, local_width), f32))
            out_specs.append(map_spec)
        return pl.pallas_call(
            functools.partial(
                backward_kernel, (here, heads, group, total, first, last, len(after))
            ),
            grid_spec=pltpu.PrefetchScalarGridSpec(
                num_scalar_prefetch=1,
                grid=(query_heads // heads,),
                in_specs=in_specs,
                out_specs=out_specs,
                scratch_shapes=scratch,
            ),
            out_shape=out_shape,
            input_output_aliases=aliases,
            **options(f"backward_{order + 1}", 12),
        )(scalars, *operands)

    pass_on([normalisers[0]] + [lse] * (pieces - 1))
    state = backward(-1, None, projected[0], after=waits(pieces - 1))
    for order in range(line - 2):
        if order:
            projected.append(projection(order, [state[3], rising[-1][0], falling[-1][0]]))
        state = backward(order, state, projected[order + 1])
        pass_on([state[3]] * pieces)

    count = line - 1
    up_map = pl.pallas_call(
        functools.partial(up_map_kernel, count),
        grid_spec=pltpu.PrefetchScalarGridSpec(
            num_scalar_prefetch=1,
            grid=(local_width // tile,),
            in_specs=[
                pl.BlockSpec((1, rank, rows), lambda n, s, j=j: (s[2 + 3 * j], 0, 0)) for j in range(count)
            ]
            + [tile_spec] * count,
            out_specs=map_spec,
        ),
        out_shape=jax.ShapeDtypeStruct((rank, local_width), f32),
        **options("up_map", 3),
    )(scalars, *([ranks] * count), *[p[2] for p in projected])
    sums = projection(line - 2, [state[3], up_map], 0, pieces - 1)
    end = projection(line - 2, [], pieces - 1, pieces, sums)
    query_gradient, key_gradient, value_gradient, down_map, up_map = backward(
        line - 2, state, end, up_map
    )
    return (
        query_gradient[None],
        key_gradient[None],
        value_gradient[None],
        down_map[None],
        up_map[None],
    )


def solution(mesh):
    placed = (
        P("pipe", "fsdp", None),
        P("pipe", "fsdp", None),
        P("pipe", None, "fsdp"),
        P("pipe", None, "fsdp"),
        P("pipe", None, "fsdp"),
        P("pipe", None, "fsdp"),
        P("pipe", None, "fsdp"),
        P("pipe", None),
    )
    return jax.shard_map(
        per_device,
        mesh=mesh,
        in_specs=placed,
        out_specs=(
            P("pipe", None, "fsdp"),
            P("pipe", None, "fsdp"),
            P("pipe", None, "fsdp"),
            P("pipe", None, "fsdp"),
            P("pipe", None, "fsdp"),
        ),
        check_vma=False,
    )
```

```python
import functools
import math

import jax
import jax.numpy as jnp
import numpy as np
from jax import lax
from jax.experimental import pallas as pl
from jax.experimental.pallas import tpu as pltpu
from jax.sharding import PartitionSpec as P

HEAD_SIZE = 128
MASKED = -1e30
LOG2E = math.log2(math.e)
VMEM_BYTES = 40 * 2**20
KEY_BLOCK = 192
QKV_AFTER = 1
FLOPS_PER_MICRO = 1.0e9

adapter_scale = 2.0


def dot_nt(a, b):
    return lax.dot_general(a, b, (((1,), (1,)), ((), ())), preferred_element_type=jnp.float32)


def dot_nn(a, b):
    return lax.dot_general(a, b, (((1,), (0,)), ((), ())), preferred_element_type=jnp.float32)


def dot_tn(a, b):
    return lax.dot_general(a, b, (((0,), (0,)), ((), ())), preferred_element_type=jnp.float32)


def three_parts(a):
    high = a.astype(jnp.bfloat16)
    rest = a - high.astype(jnp.float32)
    middle = rest.astype(jnp.bfloat16)
    low = (rest - middle.astype(jnp.float32)).astype(jnp.bfloat16)
    return jnp.concatenate([high, middle, low], axis=0)


def folded(a):
    rows = a.shape[0] // 3
    return a[:rows] + a[rows : 2 * rows] + a[2 * rows :]


def stacked_heads(a):
    count = a.shape[1] // HEAD_SIZE
    return jnp.concatenate(
        [a[:, h * HEAD_SIZE : (h + 1) * HEAD_SIZE] for h in range(count)], axis=0
    )


def key_blocks(first_key, row_start, rows):
    return first_key // KEY_BLOCK, (row_start + rows + KEY_BLOCK - 1) // KEY_BLOCK


def fill_bias(bias_ref, ids_ref, row_info_ref, low, high):
    lanes = bias_ref.shape[1]

    def one(i, _):
        at = pl.multiple_of(i * KEY_BLOCK, KEY_BLOCK)
        key_pos = at + lax.broadcasted_iota(jnp.int32, (KEY_BLOCK, lanes), 0)
        allowed = (key_pos <= row_info_ref[0, 0:1, :]) & (
            ids_ref[pl.ds(at, KEY_BLOCK), :] == row_info_ref[0, 1:2, :]
        )
        bias_ref[pl.ds(at, KEY_BLOCK), :] = jnp.where(allowed, 0.0, MASKED)
        return 0

    lax.fori_loop(low, high, one, 0)


def forward_kernel(
    grain, scalars_ref, q_ref, k_ref, v_ref, ids_ref, row_info_ref, down_ref, *rest
):
    ctx_ref, lse_ref, rank_ref, bias_ref, scores_ref, context_ref = rest[-6:]
    step = pl.program_id(1)
    rows = q_ref.shape[0]
    heads = q_ref.shape[1] // HEAD_SIZE
    row_start = pl.program_id(0) * rows
    first_key = scalars_ref[scalars_ref.shape[0] - k_ref.shape[0] // grain + row_start // grain]
    low, high = key_blocks(first_key, row_start, rows)
    lanes = heads * rows
    chunk = bias_ref.shape[1]

    @pl.when(step == 0)
    def _():
        fill_bias(bias_ref, ids_ref, row_info_ref, low, high)
        rank_ref[...] = jnp.zeros_like(rank_ref)

    stacked = stacked_heads(q_ref[...])

    def weigh(i, carry):
        top, weight = carry
        at = pl.multiple_of(i * KEY_BLOCK, KEY_BLOCK)
        keys = k_ref[pl.ds(at, KEY_BLOCK), :]
        bias = bias_ref[pl.ds(at, KEY_BLOCK), :]
        tops, weights = [], []
        for c in range(0, lanes, chunk):
            scores = dot_nt(keys, stacked[c : c + chunk]) * (LOG2E / math.sqrt(HEAD_SIZE)) + bias
            scores_ref[pl.ds(at, KEY_BLOCK), c : c + chunk] = scores
            old = top[:, c : c + chunk]
            new = jnp.maximum(old, jnp.max(scores, axis=0, keepdims=True))
            tops.append(new)
            weights.append(
                weight[:, c : c + chunk] * jnp.exp2(old - new)
                + jnp.sum(jnp.exp2(scores - new), axis=0, keepdims=True)
            )
        return jnp.concatenate(tops, axis=1), jnp.concatenate(weights, axis=1)

    top, weight = lax.fori_loop(
        low,
        high,
        weigh,
        (jnp.full((1, lanes), 2 * MASKED, jnp.float32), jnp.zeros((1, lanes), jnp.float32)),
    )
    lse = top + jnp.log(weight) * LOG2E
    lse_ref[0, 0] = lse
    context_ref[...] = jnp.zeros_like(context_ref)

    def add_values(i, _):
        at = pl.multiple_of(i * KEY_BLOCK, KEY_BLOCK)
        values = v_ref[pl.ds(at, KEY_BLOCK), :]
        for c in range(0, lanes, chunk):
            scores = scores_ref[pl.ds(at, KEY_BLOCK), c : c + chunk]
            probs = jnp.exp2(scores - lse[:, c : c + chunk]).astype(jnp.bfloat16)
            context_ref[:, c : c + chunk] += dot_tn(values, probs)
        return 0

    lax.fori_loop(low, high, add_values, 0)
    context = context_ref[...].T.astype(jnp.bfloat16)
    for h in range(heads):
        part = context[h * rows : (h + 1) * rows]
        ctx_ref[:, h * HEAD_SIZE : (h + 1) * HEAD_SIZE] = part
        rank_ref[0] += dot_nt(down_ref[:, h * HEAD_SIZE : (h + 1) * HEAD_SIZE], part)


def fetch(choice, groups, x_ref, sems):
    for c, parts in enumerate(groups):

        @pl.when(choice == c)
        def _(parts=parts):
            copies = []
            at = 0
            for p, (part, first, width) in enumerate(parts):
                copies.append(
                    pltpu.make_async_copy(
                        part.at[:, pl.ds(first, width)], x_ref.at[:, pl.ds(at, width)], sems.at[p]
                    )
                )
                at += width
            for copy in copies:
                copy.start()
            for copy in copies:
                copy.wait()


def rank_product(up_ref, x_ref, first_column):
    local = up_ref.shape[2]
    width = x_ref.shape[1]
    total = None
    for j in range(width // local):
        part = dot_nt(up_ref[first_column // local + j], x_ref[:, j * local : (j + 1) * local])
        total = part if total is None else total + part
    return total


def project(x_ref, w_ref, acc):
    width = x_ref.shape[1]
    for at in range(0, width, 4096):
        to = min(at + 4096, width)
        acc = acc + dot_nt(x_ref[:, at:to], w_ref[:, at:to])
    return acc


def rank_term(rank, down):
    return adapter_scale * dot_tn(rank, jnp.concatenate([down, down, down], axis=0))


def projection_kernel(spec, scalars_ref, *refs):
    at_choice, places, before, ends, after = spec
    refs = list(refs)

    def take(count):
        taken = refs[:count]
        del refs[:count]
        return taken

    groups = [
        [(ref, *place) for ref, place in zip(take(len(group)), group)] for group in places
    ]
    first_column = sum(columns for _, columns in places[0][:before])
    w_ref, up_ref, down_ref = take(3)
    if before:
        acc_in, rank_in = take(2)
    take(after)
    out_ref, rank_out = take(2)
    if ends:
        local_out = take(1)[0]
    x_ref, sems = take(2)
    if ends:
        parts_ref, local_ref = take(2)
    step = pl.program_id(0)

    @pl.when(step == 0)
    def _():
        fetch(scalars_ref[at_choice], [parts[before:] for parts in groups], x_ref, sems)
        rank = rank_product(up_ref, x_ref, first_column)
        rank_out[...] = rank + rank_in[...] if before else rank
        if ends:
            parts_ref[...] = three_parts(rank_out[...])
            for c, parts in enumerate(groups):
                at = 0
                for part, first, width in parts:
                    mine = scalars_ref[0] - at

                    @pl.when((scalars_ref[at_choice] == c) & (mine >= 0) & (mine < width))
                    def _(part=part, mine=mine, first=first):
                        copy = pltpu.make_async_copy(
                            part.at[:, pl.ds(pl.multiple_of(mine + first, 128), local_ref.shape[1])],
                            local_ref,
                            sems.at[0],
                        )
                        copy.start()
                        copy.wait()

                    at += width

    if ends:
        begin = rank_term(parts_ref[...], down_ref[...])
        if before:
            begin = begin + acc_in[...]
    else:
        begin = acc_in[...] if before else jnp.zeros(out_ref.shape, jnp.float32)
    out_ref[...] = project(x_ref, w_ref, begin).astype(out_ref.dtype)
    if ends:
        tile = local_out.shape[1]
        local_out[...] = local_ref[:, pl.ds(pl.multiple_of(step * tile, tile), tile)]


def up_map_kernel(count, scalars_ref, *refs):
    ranks = refs[:count]
    columns = refs[count : 2 * count]
    out_ref = refs[2 * count + 1]
    rows_total = sum(c.shape[0] for c in columns)
    scale = adapter_scale / math.sqrt(rows_total * (count + 1) // count)
    total = None
    for rank, column in zip(ranks, columns):
        part = folded(dot_nn(three_parts(rank[0]), column[...]))
        total = part if total is None else total + part
    out_ref[...] = scale * total


def backward_kernel(spec, scalars_ref, *refs):
    here, grain, first, last, after = spec
    refs = list(refs)

    def take(count):
        taken = refs[:count]
        del refs[:count]
        return taken

    if last:
        local_ref, rank_ctx_ref, um_in = take(3)
    grad_ref, rank_in, q_ref, ctx_ref, k_ref, v_ref, ids_ref, row_info_ref, lse_ref = take(9)
    if not first:
        _, dk_in, dv_in, dm_in = take(4)
    take(after)
    dq_ref, dk_ref, dv_ref, dm_ref = take(4)
    if last:
        um_ref = take(1)[0]
    bias_ref, parts_ref, dk_sum, dv_sum, probs_ref, grad_scores_ref, grad_q_ref = take(7)

    step = pl.program_id(0)
    total = k_ref.shape[0]
    rows = q_ref.shape[0]
    heads = q_ref.shape[1] // HEAD_SIZE
    lanes = heads * rows
    chunk = bias_ref.shape[1]
    row_start = scalars_ref[here] * rows
    first_key = scalars_ref[scalars_ref.shape[0] - total // grain + row_start // grain]
    low, high = key_blocks(first_key, row_start, rows)
    gradient_scale = adapter_scale / math.sqrt(total)
    inv_scale = 1.0 / math.sqrt(HEAD_SIZE)

    @pl.when(step == 0)
    def _():
        parts_ref[...] = three_parts(rank_in[...])
        fill_bias(bias_ref, ids_ref, row_info_ref, low, high)

    if first:
        dk_sum[...] = jnp.zeros_like(dk_sum)
        dv_sum[...] = jnp.zeros_like(dv_sum)
    else:
        dk_sum[...] = dk_in[...]
        dv_sum[...] = dv_in[...]
    grad_q_ref[...] = jnp.zeros_like(grad_q_ref)
    queries = stacked_heads(q_ref[...])
    grads = stacked_heads(grad_ref[...])
    delta = jnp.sum(
        (grads.astype(jnp.float32) * stacked_heads(ctx_ref[...]).astype(jnp.float32)).T,
        axis=0,
        keepdims=True,
    )

    def one(i, _):
        at = pl.multiple_of(i * KEY_BLOCK, KEY_BLOCK)
        keys = k_ref[pl.ds(at, KEY_BLOCK), :]
        values = v_ref[pl.ds(at, KEY_BLOCK), :]
        bias = bias_ref[pl.ds(at, KEY_BLOCK), :]
        for c in range(0, lanes, chunk):
            here = slice(c, c + chunk)
            scores = dot_nt(keys, queries[here]) * (LOG2E * inv_scale) + bias
            probs = jnp.exp2(scores - lse_ref[0, 0, :, here])
            grad_probs = dot_nt(values, grads[here])
            probs_ref[:, here] = probs.astype(jnp.bfloat16)
            grad_scores_ref[:, here] = (probs * (grad_probs - delta[:, here])).astype(jnp.bfloat16)
        grad_scores = grad_scores_ref[...]
        dk_sum[pl.ds(at, KEY_BLOCK), :] += dot_nn(grad_scores, queries) * inv_scale
        dv_sum[pl.ds(at, KEY_BLOCK), :] += dot_nn(probs_ref[...], grads)
        grad_q_ref[...] += dot_tn(keys, grad_scores)
        return 0

    lax.fori_loop(low, high, one, 0)
    dk_ref[...] = dk_sum[...].astype(dk_ref.dtype)
    dv_ref[...] = dv_sum[...].astype(dv_ref.dtype)
    grad_q = (grad_q_ref[...] * inv_scale).T.astype(jnp.bfloat16)
    for h in range(heads):
        dq_ref[:, h * HEAD_SIZE : (h + 1) * HEAD_SIZE] = grad_q[h * rows : (h + 1) * rows]

    down_part = gradient_scale * folded(dot_nn(parts_ref[...], ctx_ref[...]))
    dm_ref[...] = down_part if first else dm_in[...] + down_part
    if last:
        um_ref[...] = um_in[...] + gradient_scale * folded(
            dot_nn(three_parts(rank_ctx_ref[0]), local_ref[...])
        )


def options(name, micros, axes=1):
    return dict(
        compiler_params=pltpu.CompilerParams(
            dimension_semantics=("arbitrary",) * axes, vmem_limit_bytes=VMEM_BYTES
        ),
        cost_estimate=pl.CostEstimate(
            flops=int(micros * FLOPS_PER_MICRO), bytes_accessed=1, transcendentals=0
        ),
        name=name,
    )


ANYWHERE = pl.BlockSpec(memory_space=pl.ANY)


def per_device(
    handoff_gradient,
    output_weight,
    adapter_down,
    adapter_up,
    stored_queries,
    stored_keys,
    stored_values,
    segments,
):
    pipe_count = lax.axis_size("pipe")
    line = lax.axis_size("fsdp")
    member = lax.axis_index("fsdp")
    shard = handoff_gradient.shape[1]
    total = shard * line
    model_width = handoff_gradient.shape[2]
    query_width = stored_queries.shape[2]
    kv_width = stored_keys.shape[2]
    rank = adapter_down.shape[1]
    query_heads = query_width // HEAD_SIZE
    kv_heads = kv_width // HEAD_SIZE
    group = query_heads // kv_heads
    local_width = adapter_up.shape[2]
    bf16, f32 = jnp.bfloat16, jnp.float32
    weight = output_weight[0]
    down = adapter_down[0]

    def spread(block):
        blocks = [block]
        for d in range(1, line):
            route = [(i, (i + d) % line) for i in range(line)]
            blocks.append(lax.ppermute(block, "fsdp", route))
        turned = jnp.stack(blocks[::-1] + blocks[::-1])
        return lax.dynamic_slice_in_dim(turned, line - 1 - member, line, 0)

    from_next = [((i + 1) % pipe_count, i) for i in range(pipe_count)]
    mirrored = [(i, pipe_count - 1 - i) for i in range(pipe_count)]
    widths = [model_width // 2, model_width // 2]
    own, at = [], 0
    for width in widths:
        part = handoff_gradient[0, :, at : at + width]
        if own:
            part, _ = lax.optimization_barrier((part, own[-1]))
        else:
            first_part = part
        own.append(lax.ppermute(part, "pipe", from_next))
        at += width
    saved = lax.optimization_barrier(
        (stored_queries[0], stored_keys[0], stored_values[0], first_part)
    )[:3]
    packed = jnp.concatenate(saved, axis=1)
    up_all = spread(lax.optimization_barrier((adapter_up[0], packed))[0])
    rising, falling = [own], [own]
    crossing = {}

    def after(part, token):
        return part if token is None else lax.optimization_barrier((part, token))[0]

    def pass_on(token):
        k = len(rising)
        if k >= line:
            return
        up_pairs = [(i, i + 1) for i in range(k - 1, line - 1)]
        down_pairs = [(i + 1, i) for i in range(line - k)]
        rising.append([lax.ppermute(after(p, token), "fsdp", up_pairs) for p in rising[-1]])
        falling.append([lax.ppermute(after(p, token), "fsdp", down_pairs) for p in falling[-1]])

    def cross(piece, kind, token):
        routes = {
            "near": [(1, 0), (2, 3)],
            "middle": [(1, 2), (2, 1)],
            "far": [(1, 3), (2, 0)],
        }
        rose, fell = rising[1][piece], falling[1][piece]
        first = member == (2 if kind == "near" else 1)
        part = jnp.where(first, rose, fell)
        crossing.setdefault(kind, []).append(
            lax.ppermute(after(part, token), "fsdp", routes[kind])
        )

    pass_on(None)
    packed, _ = lax.optimization_barrier((packed, own[QKV_AFTER]))
    packed = lax.ppermute(packed, "pipe", mirrored)

    def arrival(device, order):
        found = []
        for k in range(1, line):
            if device >= k:
                found.append((k, True, device - k))
            if device + k < line:
                found.append((k, False, device + k))
        return found[order]

    def groups_of(order):
        if order < 0:
            return ["own"]
        return sorted({carrier(d, order) for d in range(line)})

    def carrier(device, order):
        if order < 0:
            return "own"
        k, rises, _ = arrival(device, order)
        if line == 4 and k > 1:
            return "far" if k == 3 else "near" if device in (0, 3) else "middle"
        return f"{'rising' if rises else 'falling'} {k}"

    def choices(order):
        groups = []
        for name in groups_of(order):
            if name == "own":
                parts = own
            elif name in crossing:
                parts = crossing[name]
            else:
                way, k = name.split()
                parts = (rising if way == "rising" else falling)[int(k)]
            groups.append([(part, 0, part.shape[1]) for part in parts])
        return groups

    rows_f = total // 4
    grain = math.gcd(rows_f, shard)
    table = np.zeros((line, 1 + 2 * line), np.int32)
    for d in range(line):
        table[d, 0] = d * local_width
        for order in range(-1, line - 1):
            owner = d if order < 0 else arrival(d, order)[2]
            at = 3 + 2 * order
            table[d, at : at + 2] = groups_of(order).index(carrier(d, order)), owner
    ids = segments[0]
    first_keys = jnp.sum(ids[None, :] < ids[::grain, None], axis=1, dtype=jnp.int32)
    scalars = jnp.concatenate(
        [lax.dynamic_index_in_dim(jnp.asarray(table), member, 0, keepdims=False), first_keys]
    )

    tile_p = min(512, query_width)

    def projection(order, after, low=0, high=None, sums=()):
        groups = choices(order)
        high = len(groups[0]) if high is None else high
        ends = high == len(groups[0])
        groups = [parts[:high] for parts in groups]
        offsets = [0]
        for _, _, columns in groups[0]:
            offsets.append(offsets[-1] + columns)
        places = [[(first, columns) for _, first, columns in parts] for parts in groups]
        width = offsets[high] - offsets[low]
        block, odd = divmod(offsets[low], width)
        assert odd == 0
        operands = [part for parts in groups for part, _, _ in parts]
        in_specs = [ANYWHERE] * len(operands)
        rank_spec = pl.BlockSpec((rank, shard), lambda n, s: (0, 0))
        tile_spec = pl.BlockSpec((shard, tile_p), lambda n, s: (0, n))
        operands += [weight, up_all, down, *sums, *after]
        in_specs += [
            pl.BlockSpec((tile_p, width), lambda n, s: (n, block)),
            pl.BlockSpec((line, rank, local_width), lambda n, s: (0, 0, 0)),
            pl.BlockSpec((rank, tile_p), lambda n, s: (0, n)),
        ]
        in_specs += [tile_spec, rank_spec][: len(sums)] + [ANYWHERE] * len(after)
        out_shape = [
            jax.ShapeDtypeStruct((shard, query_width), bf16 if ends else f32),
            jax.ShapeDtypeStruct((rank, shard), f32),
        ]
        out_specs = [tile_spec, rank_spec]
        scratch = [
            pltpu.VMEM((shard, width), bf16),
            pltpu.SemaphoreType.DMA((high - low,)),
        ]
        if ends:
            out_shape.append(jax.ShapeDtypeStruct((shard, local_width), bf16))
            out_specs.append(
                pl.BlockSpec((shard, local_width * tile_p // query_width), lambda n, s: (0, n))
            )
            scratch.append(pltpu.VMEM((3 * rank, shard), bf16))
            scratch.append(pltpu.VMEM((shard, local_width), bf16))
        return pl.pallas_call(
            functools.partial(
                projection_kernel, (3 + 2 * order, places, low, ends, len(after))
            ),
            grid_spec=pltpu.PrefetchScalarGridSpec(
                num_scalar_prefetch=1,
                grid=(query_width // tile_p,),
                in_specs=in_specs,
                out_specs=out_specs,
                scratch_shapes=scratch,
            ),
            out_shape=out_shape,
            **options(f"projection_{order + 1}_{high}", 18 * width / model_width),
        )(scalars, *operands)

    projected = [projection(-1, [])]
    done_before = projected[0][1]
    if line == 4:
        cross(0, "near", done_before)
        cross(0, "middle", done_before)
        cross(1, "near", done_before)
        cross(1, "middle", done_before)
    else:
        pass_on(done_before)
    if line > 2:
        projected.append(projection(0, [done_before]))
        done_before = projected[1][1]

    ids_column = ids[:, None]
    lanes_f = group * rows_f
    chunk_f = 2 * rows_f if group % 2 == 0 else rows_f

    def row_info(rows, heads):
        pos = jnp.arange(total, dtype=jnp.int32).reshape(total // rows, 1, rows)
        row_ids = ids.reshape(total // rows, 1, rows)
        both = jnp.concatenate([pos, row_ids], axis=1)
        return jnp.tile(both, (1, 1, heads))

    wide = group * HEAD_SIZE
    pins = [crossing["near"][0], crossing["middle"][0]] if line == 4 else []
    key_at, value_at = query_heads, query_heads + kv_heads
    context, lse, rank_portion = pl.pallas_call(
        functools.partial(forward_kernel, grain),
        grid_spec=pltpu.PrefetchScalarGridSpec(
            num_scalar_prefetch=1,
            grid=(4, kv_heads),
            in_specs=[
                pl.BlockSpec((rows_f, wide), lambda b, n, s: (b, n)),
                pl.BlockSpec((total, HEAD_SIZE), lambda b, n, s: (0, key_at + n)),
                pl.BlockSpec((total, HEAD_SIZE), lambda b, n, s: (0, value_at + n)),
                pl.BlockSpec((total, 1), lambda b, n, s: (0, 0)),
                pl.BlockSpec((1, 2, chunk_f), lambda b, n, s: (b, 0, 0)),
                pl.BlockSpec((rank, wide), lambda b, n, s: (0, n)),
                ANYWHERE,
            ]
            + [ANYWHERE] * len(pins),
            out_specs=[
                pl.BlockSpec((rows_f, wide), lambda b, n, s: (b, n)),
                pl.BlockSpec((1, 1, 1, lanes_f), lambda b, n, s: (b, n, 0, 0)),
                pl.BlockSpec((1, rank, rows_f), lambda b, n, s: (b, 0, 0)),
            ],
            scratch_shapes=[
                pltpu.VMEM((total, chunk_f), f32),
                pltpu.VMEM((total, lanes_f), f32),
                pltpu.VMEM((HEAD_SIZE, lanes_f), f32),
            ],
        ),
        out_shape=[
            jax.ShapeDtypeStruct((total, query_width), bf16),
            jax.ShapeDtypeStruct((4, kv_heads, 1, lanes_f), f32),
            jax.ShapeDtypeStruct((4, rank, rows_f), f32),
        ],
        **options("forward", 20, 2),
    )(scalars, packed, packed, packed, ids_column, row_info(rows_f, chunk_f // rows_f), down, done_before, *pins)

    rank_context = rank_portion
    for d in range(1, line):
        route = [(i, (i + d) % line) for i in range(line)]
        rank_context = rank_context + lax.ppermute(rank_portion, "fsdp", route)

    rows = shard
    heads = group
    chunk = rows * max(h for h in range(1, group + 1) if group % h == 0 and (h == 1 or h * rows <= 384))
    normal = (
        lse.reshape(4, query_heads, rows_f // rows, rows)
        .transpose(0, 2, 1, 3)
        .reshape(total // rows, query_heads // heads, 1, heads * rows)
    )
    ranks = (
        rank_context.reshape(4, rank, rows_f // rows, rows)
        .transpose(0, 2, 1, 3)
        .reshape(total // rows, rank, rows)
    )
    info = row_info(rows, chunk // rows)
    tile = heads * HEAD_SIZE
    lanes = heads * rows
    kv_spec = pl.BlockSpec((total, HEAD_SIZE), lambda n, s: (0, n))
    tile_spec = pl.BlockSpec((rows, tile), lambda n, s: (0, n))
    map_spec = pl.BlockSpec((rank, tile), lambda n, s: (0, n))
    rank_spec = pl.BlockSpec((rank, rows), lambda n, s: (0, 0))

    def backward(order, state, source, up_map=None, after=()):
        first = state is None
        last = up_map is not None
        here = 4 + 2 * order
        row_spec = pl.BlockSpec((rows, tile), lambda n, s: (s[here], n))
        ctx_rank_spec = pl.BlockSpec((1, rank, rows), lambda n, s: (s[here], 0, 0))
        operands, in_specs = [], []
        grad, rank_grad, local_columns = source
        if last:
            operands += [local_columns, ranks, up_map]
            in_specs += [tile_spec, ctx_rank_spec, map_spec]
        operands += [
            grad,
            rank_grad,
            packed,
            context,
            packed,
            packed,
            ids_column,
            info,
            normal,
        ]
        in_specs += [
            tile_spec,
            rank_spec,
            row_spec,
            row_spec,
            pl.BlockSpec((total, HEAD_SIZE), lambda n, s: (0, key_at + n)),
            pl.BlockSpec((total, HEAD_SIZE), lambda n, s: (0, value_at + n)),
            pl.BlockSpec((total, 1), lambda n, s: (0, 0)),
            pl.BlockSpec((1, 2, chunk), lambda n, s: (s[here], 0, 0)),
            pl.BlockSpec((1, 1, 1, lanes), lambda n, s: (s[here], n, 0, 0)),
        ]
        aliases = {}
        if not first:
            aliases[1 + len(operands)] = 0
            operands += list(state)
            in_specs += [ANYWHERE, kv_spec, kv_spec, map_spec]
        operands += list(after)
        in_specs += [ANYWHERE] * len(after)
        kv_type = bf16 if last else f32
        out_shape = [
            jax.ShapeDtypeStruct((total, query_width), bf16),
            jax.ShapeDtypeStruct((total, kv_width), kv_type),
            jax.ShapeDtypeStruct((total, kv_width), kv_type),
            jax.ShapeDtypeStruct((rank, query_width), f32),
        ]
        out_specs = [row_spec, kv_spec, kv_spec, map_spec]
        scratch = [
            pltpu.VMEM((total, chunk), f32),
            pltpu.VMEM((3 * rank, rows), bf16),
            pltpu.VMEM((total, HEAD_SIZE), f32),
            pltpu.VMEM((total, HEAD_SIZE), f32),
            pltpu.VMEM((KEY_BLOCK, lanes), bf16),
            pltpu.VMEM((KEY_BLOCK, lanes), bf16),
            pltpu.VMEM((HEAD_SIZE, lanes), f32),
        ]
        if last:
            out_shape.append(jax.ShapeDtypeStruct((rank, local_width), f32))
            out_specs.append(map_spec)
        return pl.pallas_call(
            functools.partial(
                backward_kernel, (here, grain, first, last, len(after))
            ),
            grid_spec=pltpu.PrefetchScalarGridSpec(
                num_scalar_prefetch=1,
                grid=(query_heads // heads,),
                in_specs=in_specs,
                out_specs=out_specs,
                scratch_shapes=scratch,
            ),
            out_shape=out_shape,
            input_output_aliases=aliases,
            **options(f"backward_{order + 1}", 8),
        )(scalars, *operands)

    if line == 4:
        cross(0, "far", lse)
    else:
        pass_on(lse)
    state = backward(-1, None, projected[0])
    for order in range(line - 2):
        if order:
            projected.append(projection(order, [state[3]]))
        pins = [crossing["near"][1]] if line == 4 and order == 0 else []
        state = backward(order, state, projected[order + 1], after=pins)
        if line != 4:
            pass_on(state[3])
        elif order == 0:
            cross(1, "far", state[3])

    sums = projection(line - 2, [state[3]], 0, 1)

    count = line - 1
    up_map = pl.pallas_call(
        functools.partial(up_map_kernel, count),
        grid_spec=pltpu.PrefetchScalarGridSpec(
            num_scalar_prefetch=1,
            grid=(local_width // tile,),
            in_specs=[
                pl.BlockSpec((1, rank, rows), lambda n, s, j=j: (s[2 + 2 * j], 0, 0)) for j in range(count)
            ]
            + [tile_spec] * count
            + [ANYWHERE],
            out_specs=map_spec,
        ),
        out_shape=jax.ShapeDtypeStruct((rank, local_width), f32),
        **options("up_map", 3),
    )(scalars, *([ranks] * count), *[p[2] for p in projected], sums[1])
    end = projection(line - 2, [], 1, 2, sums)
    query_gradient, key_gradient, value_gradient, down_map, up_map = backward(
        line - 2, state, end, up_map
    )
    return (
        query_gradient[None],
        key_gradient[None],
        value_gradient[None],
        down_map[None],
        up_map[None],
    )


def solution(mesh):
    placed = (
        P("pipe", "fsdp", None),
        P("pipe", "fsdp", None),
        P("pipe", None, "fsdp"),
        P("pipe", None, "fsdp"),
        P("pipe", None, "fsdp"),
        P("pipe", None, "fsdp"),
        P("pipe", None, "fsdp"),
        P("pipe", None),
    )
    return jax.shard_map(
        per_device,
        mesh=mesh,
        in_specs=placed,
        out_specs=(
            P("pipe", None, "fsdp"),
            P("pipe", None, "fsdp"),
            P("pipe", None, "fsdp"),
            P("pipe", None, "fsdp"),
            P("pipe", None, "fsdp"),
        ),
        check_vma=False,
    )
```

```python
import functools
import math

import jax
import jax.numpy as jnp
import numpy as np
from jax import lax
from jax.experimental import pallas as pl
from jax.experimental.pallas import tpu as pltpu
from jax.sharding import PartitionSpec as P

HEAD_SIZE = 128
MASKED = -1e30
LOG2E = math.log2(math.e)
VMEM_BYTES = 40 * 2**20
KEY_BLOCK = 192
QKV_AFTER = 1
FLOPS_PER_MICRO = 1.0e9

adapter_scale = 2.0


def dot_nt(a, b):
    return lax.dot_general(a, b, (((1,), (1,)), ((), ())), preferred_element_type=jnp.float32)


def dot_nn(a, b):
    return lax.dot_general(a, b, (((1,), (0,)), ((), ())), preferred_element_type=jnp.float32)


def dot_tn(a, b):
    return lax.dot_general(a, b, (((0,), (0,)), ((), ())), preferred_element_type=jnp.float32)


def three_parts(a):
    high = a.astype(jnp.bfloat16)
    rest = a - high.astype(jnp.float32)
    middle = rest.astype(jnp.bfloat16)
    low = (rest - middle.astype(jnp.float32)).astype(jnp.bfloat16)
    return jnp.concatenate([high, middle, low], axis=0)


def folded(a):
    rows = a.shape[0] // 3
    return a[:rows] + a[rows : 2 * rows] + a[2 * rows :]


def stacked_heads(a):
    count = a.shape[1] // HEAD_SIZE
    return jnp.concatenate(
        [a[:, h * HEAD_SIZE : (h + 1) * HEAD_SIZE] for h in range(count)], axis=0
    )


def key_blocks(first_key, row_start, rows):
    return first_key // KEY_BLOCK, (row_start + rows + KEY_BLOCK - 1) // KEY_BLOCK


def fill_bias(bias_ref, ids_ref, row_info_ref, low, high):
    lanes = bias_ref.shape[1]

    def one(i, _):
        at = pl.multiple_of(i * KEY_BLOCK, KEY_BLOCK)
        key_pos = at + lax.broadcasted_iota(jnp.int32, (KEY_BLOCK, lanes), 0)
        allowed = (key_pos <= row_info_ref[0, 0:1, :]) & (
            ids_ref[pl.ds(at, KEY_BLOCK), :] == row_info_ref[0, 1:2, :]
        )
        bias_ref[pl.ds(at, KEY_BLOCK), :] = jnp.where(allowed, 0.0, MASKED)
        return 0

    lax.fori_loop(low, high, one, 0)


def forward_kernel(
    grain, scalars_ref, q_ref, k_ref, v_ref, ids_ref, row_info_ref, down_ref, *rest
):
    ctx_ref, lse_ref, rank_ref, bias_ref, scores_ref, context_ref = rest[-6:]
    step = pl.program_id(1)
    rows = q_ref.shape[0]
    heads = q_ref.shape[1] // HEAD_SIZE
    row_start = pl.program_id(0) * rows
    first_key = scalars_ref[scalars_ref.shape[0] - k_ref.shape[0] // grain + row_start // grain]
    low, high = key_blocks(first_key, row_start, rows)
    lanes = heads * rows
    chunk = bias_ref.shape[1]

    @pl.when(step == 0)
    def _():
        fill_bias(bias_ref, ids_ref, row_info_ref, low, high)
        rank_ref[...] = jnp.zeros_like(rank_ref)

    stacked = stacked_heads(q_ref[...])

    def weigh(i, carry):
        top, weight = carry
        at = pl.multiple_of(i * KEY_BLOCK, KEY_BLOCK)
        keys = k_ref[pl.ds(at, KEY_BLOCK), :]
        bias = bias_ref[pl.ds(at, KEY_BLOCK), :]
        tops, weights = [], []
        for c in range(0, lanes, chunk):
            scores = dot_nt(keys, stacked[c : c + chunk]) * (LOG2E / math.sqrt(HEAD_SIZE)) + bias
            scores_ref[pl.ds(at, KEY_BLOCK), c : c + chunk] = scores
            old = top[:, c : c + chunk]
            new = jnp.maximum(old, jnp.max(scores, axis=0, keepdims=True))
            tops.append(new)
            weights.append(
                weight[:, c : c + chunk] * jnp.exp2(old - new)
                + jnp.sum(jnp.exp2(scores - new), axis=0, keepdims=True)
            )
        return jnp.concatenate(tops, axis=1), jnp.concatenate(weights, axis=1)

    top, weight = lax.fori_loop(
        low,
        high,
        weigh,
        (jnp.full((1, lanes), 2 * MASKED, jnp.float32), jnp.zeros((1, lanes), jnp.float32)),
    )
    lse = top + jnp.log(weight) * LOG2E
    lse_ref[0, 0] = lse
    context_ref[...] = jnp.zeros_like(context_ref)

    def add_values(i, _):
        at = pl.multiple_of(i * KEY_BLOCK, KEY_BLOCK)
        values = v_ref[pl.ds(at, KEY_BLOCK), :]
        for c in range(0, lanes, chunk):
            scores = scores_ref[pl.ds(at, KEY_BLOCK), c : c + chunk]
            probs = jnp.exp2(scores - lse[:, c : c + chunk]).astype(jnp.bfloat16)
            context_ref[:, c : c + chunk] += dot_tn(values, probs)
        return 0

    lax.fori_loop(low, high, add_values, 0)
    context = context_ref[...].T.astype(jnp.bfloat16)
    for h in range(heads):
        part = context[h * rows : (h + 1) * rows]
        ctx_ref[:, h * HEAD_SIZE : (h + 1) * HEAD_SIZE] = part
        rank_ref[0] += dot_nt(down_ref[:, h * HEAD_SIZE : (h + 1) * HEAD_SIZE], part)


def fetch(choice, groups, x_ref, sems):
    for c, parts in enumerate(groups):

        @pl.when(choice == c)
        def _(parts=parts):
            copies = []
            at = 0
            for p, (part, first, width) in enumerate(parts):
                copies.append(
                    pltpu.make_async_copy(
                        part.at[:, pl.ds(first, width)], x_ref.at[:, pl.ds(at, width)], sems.at[p]
                    )
                )
                at += width
            for copy in copies:
                copy.start()
            for copy in copies:
                copy.wait()


def rank_product(up_ref, x_ref, first_column):
    local = up_ref.shape[2]
    width = x_ref.shape[1]
    total = None
    for j in range(width // local):
        part = dot_nt(up_ref[first_column // local + j], x_ref[:, j * local : (j + 1) * local])
        total = part if total is None else total + part
    return total


def project(x_ref, w_ref, acc):
    width = x_ref.shape[1]
    for at in range(0, width, 4096):
        to = min(at + 4096, width)
        acc = acc + dot_nt(x_ref[:, at:to], w_ref[:, at:to])
    return acc


def rank_term(rank, down):
    return adapter_scale * dot_tn(rank, jnp.concatenate([down, down, down], axis=0))


def projection_kernel(spec, scalars_ref, *refs):
    at_choice, places, before, ends, after = spec
    refs = list(refs)

    def take(count):
        taken = refs[:count]
        del refs[:count]
        return taken

    groups = [
        [(ref, *place) for ref, place in zip(take(len(group)), group)] for group in places
    ]
    first_column = sum(columns for _, columns in places[0][:before])
    w_ref, up_ref, down_ref = take(3)
    if before:
        acc_in, rank_in = take(2)
    take(after)
    out_ref, rank_out = take(2)
    if ends:
        local_out = take(1)[0]
    x_ref, sems = take(2)
    if ends:
        parts_ref, local_ref = take(2)
    step = pl.program_id(0)

    @pl.when(step == 0)
    def _():
        fetch(scalars_ref[at_choice], [parts[before:] for parts in groups], x_ref, sems)
        rank = rank_product(up_ref, x_ref, first_column)
        rank_out[...] = rank + rank_in[...] if before else rank
        if ends:
            parts_ref[...] = three_parts(rank_out[...])
            for c, parts in enumerate(groups):
                at = 0
                for part, first, width in parts:
                    mine = scalars_ref[0] - at

                    @pl.when((scalars_ref[at_choice] == c) & (mine >= 0) & (mine < width))
                    def _(part=part, mine=mine, first=first):
                        copy = pltpu.make_async_copy(
                            part.at[:, pl.ds(pl.multiple_of(mine + first, 128), local_ref.shape[1])],
                            local_ref,
                            sems.at[0],
                        )
                        copy.start()
                        copy.wait()

                    at += width

    if ends:
        begin = rank_term(parts_ref[...], down_ref[...])
        if before:
            begin = begin + acc_in[...]
    else:
        begin = acc_in[...] if before else jnp.zeros(out_ref.shape, jnp.float32)
    out_ref[...] = project(x_ref, w_ref, begin).astype(out_ref.dtype)
    if ends:
        tile = local_out.shape[1]
        local_out[...] = local_ref[:, pl.ds(pl.multiple_of(step * tile, tile), tile)]


def up_map_kernel(count, scalars_ref, *refs):
    ranks = refs[:count]
    columns = refs[count : 2 * count]
    out_ref = refs[2 * count + 1]
    rows_total = sum(c.shape[0] for c in columns)
    scale = adapter_scale / math.sqrt(rows_total * (count + 1) // count)
    total = None
    for rank, column in zip(ranks, columns):
        part = folded(dot_nn(three_parts(rank[0]), column[...]))
        total = part if total is None else total + part
    out_ref[...] = scale * total


def backward_kernel(spec, scalars_ref, *refs):
    here, grain, first, last, after = spec
    refs = list(refs)

    def take(count):
        taken = refs[:count]
        del refs[:count]
        return taken

    if last:
        local_ref, rank_ctx_ref, um_in = take(3)
    grad_ref, rank_in, q_ref, ctx_ref, k_ref, v_ref, ids_ref, row_info_ref, lse_ref = take(9)
    if not first:
        _, dk_in, dv_in, dm_in = take(4)
    take(after)
    dq_ref, dk_ref, dv_ref, dm_ref = take(4)
    if last:
        um_ref = take(1)[0]
    bias_ref, parts_ref, dk_sum, dv_sum, probs_ref, grad_scores_ref, grad_q_ref = take(7)

    step = pl.program_id(0)
    total = k_ref.shape[0]
    rows = q_ref.shape[0]
    heads = q_ref.shape[1] // HEAD_SIZE
    lanes = heads * rows
    chunk = bias_ref.shape[1]
    row_start = scalars_ref[here] * rows
    first_key = scalars_ref[scalars_ref.shape[0] - total // grain + row_start // grain]
    low, high = key_blocks(first_key, row_start, rows)
    gradient_scale = adapter_scale / math.sqrt(total)
    inv_scale = 1.0 / math.sqrt(HEAD_SIZE)

    @pl.when(step == 0)
    def _():
        parts_ref[...] = three_parts(rank_in[...])
        fill_bias(bias_ref, ids_ref, row_info_ref, low, high)

    if first:
        dk_sum[...] = jnp.zeros_like(dk_sum)
        dv_sum[...] = jnp.zeros_like(dv_sum)
    else:
        dk_sum[...] = dk_in[...]
        dv_sum[...] = dv_in[...]
    grad_q_ref[...] = jnp.zeros_like(grad_q_ref)
    queries = stacked_heads(q_ref[...])
    grads = stacked_heads(grad_ref[...])
    delta = jnp.sum(
        (grads.astype(jnp.float32) * stacked_heads(ctx_ref[...]).astype(jnp.float32)).T,
        axis=0,
        keepdims=True,
    )

    def one(i, _):
        at = pl.multiple_of(i * KEY_BLOCK, KEY_BLOCK)
        keys = k_ref[pl.ds(at, KEY_BLOCK), :]
        values = v_ref[pl.ds(at, KEY_BLOCK), :]
        bias = bias_ref[pl.ds(at, KEY_BLOCK), :]
        for c in range(0, lanes, chunk):
            here = slice(c, c + chunk)
            scores = dot_nt(keys, queries[here]) * (LOG2E * inv_scale) + bias
            probs = jnp.exp2(scores - lse_ref[0, 0, :, here])
            grad_probs = dot_nt(values, grads[here])
            probs_ref[:, here] = probs.astype(jnp.bfloat16)
            grad_scores_ref[:, here] = (probs * (grad_probs - delta[:, here])).astype(jnp.bfloat16)
        grad_scores = grad_scores_ref[...]
        dk_sum[pl.ds(at, KEY_BLOCK), :] += dot_nn(grad_scores, queries) * inv_scale
        dv_sum[pl.ds(at, KEY_BLOCK), :] += dot_nn(probs_ref[...], grads)
        grad_q_ref[...] += dot_tn(keys, grad_scores)
        return 0

    lax.fori_loop(low, high, one, 0)
    dk_ref[...] = dk_sum[...].astype(dk_ref.dtype)
    dv_ref[...] = dv_sum[...].astype(dv_ref.dtype)
    grad_q = (grad_q_ref[...] * inv_scale).T.astype(jnp.bfloat16)
    for h in range(heads):
        dq_ref[:, h * HEAD_SIZE : (h + 1) * HEAD_SIZE] = grad_q[h * rows : (h + 1) * rows]

    down_part = gradient_scale * folded(dot_nn(parts_ref[...], ctx_ref[...]))
    dm_ref[...] = down_part if first else dm_in[...] + down_part
    if last:
        um_ref[...] = um_in[...] + gradient_scale * folded(
            dot_nn(three_parts(rank_ctx_ref[0]), local_ref[...])
        )


def options(name, micros, axes=1):
    return dict(
        compiler_params=pltpu.CompilerParams(
            dimension_semantics=("arbitrary",) * axes, vmem_limit_bytes=VMEM_BYTES
        ),
        cost_estimate=pl.CostEstimate(
            flops=int(micros * FLOPS_PER_MICRO), bytes_accessed=1, transcendentals=0
        ),
        name=name,
    )


ANYWHERE = pl.BlockSpec(memory_space=pl.ANY)


def per_device(
    handoff_gradient,
    output_weight,
    adapter_down,
    adapter_up,
    stored_queries,
    stored_keys,
    stored_values,
    segments,
):
    pipe_count = lax.axis_size("pipe")
    line = lax.axis_size("fsdp")
    member = lax.axis_index("fsdp")
    shard = handoff_gradient.shape[1]
    total = shard * line
    model_width = handoff_gradient.shape[2]
    query_width = stored_queries.shape[2]
    kv_width = stored_keys.shape[2]
    rank = adapter_down.shape[1]
    query_heads = query_width // HEAD_SIZE
    kv_heads = kv_width // HEAD_SIZE
    group = query_heads // kv_heads
    local_width = adapter_up.shape[2]
    bf16, f32 = jnp.bfloat16, jnp.float32
    weight = output_weight[0]
    down = adapter_down[0]

    def spread(block):
        blocks = [block]
        for d in range(1, line):
            route = [(i, (i + d) % line) for i in range(line)]
            blocks.append(lax.ppermute(block, "fsdp", route))
        turned = jnp.stack(blocks[::-1] + blocks[::-1])
        return lax.dynamic_slice_in_dim(turned, line - 1 - member, line, 0)

    from_next = [((i + 1) % pipe_count, i) for i in range(pipe_count)]
    mirrored = [(i, pipe_count - 1 - i) for i in range(pipe_count)]
    widths = [model_width // 2, model_width // 2]
    own, at = [], 0
    for width in widths:
        part = handoff_gradient[0, :, at : at + width]
        if own:
            part, _ = lax.optimization_barrier((part, own[-1]))
        own.append(lax.ppermute(part, "pipe", from_next))
        at += width
    packed = jnp.concatenate([stored_queries[0], stored_keys[0], stored_values[0]], axis=1)
    up_all = spread(lax.optimization_barrier((adapter_up[0], own[0]))[0])
    rising, falling = [own], [own]
    crossing = {}

    def after(part, token):
        return part if token is None else lax.optimization_barrier((part, token))[0]

    def pass_on(token):
        k = len(rising)
        if k >= line:
            return
        up_pairs = [(i, i + 1) for i in range(k - 1, line - 1)]
        down_pairs = [(i + 1, i) for i in range(line - k)]
        rising.append([lax.ppermute(after(p, token), "fsdp", up_pairs) for p in rising[-1]])
        falling.append([lax.ppermute(after(p, token), "fsdp", down_pairs) for p in falling[-1]])

    def cross(piece, kind, token):
        routes = {
            "near": [(1, 0), (2, 3)],
            "middle": [(1, 2), (2, 1)],
            "far": [(1, 3), (2, 0)],
        }
        rose, fell = rising[1][piece], falling[1][piece]
        first = member == (2 if kind == "near" else 1)
        part = jnp.where(first, rose, fell)
        crossing.setdefault(kind, []).append(
            lax.ppermute(after(part, token), "fsdp", routes[kind])
        )

    pass_on(None)
    packed, _ = lax.optimization_barrier((packed, own[QKV_AFTER]))
    packed = lax.ppermute(packed, "pipe", mirrored)

    def arrival(device, order):
        found = []
        for k in range(1, line):
            if device >= k:
                found.append((k, True, device - k))
            if device + k < line:
                found.append((k, False, device + k))
        return found[order]

    def groups_of(order):
        if order < 0:
            return ["own"]
        return sorted({carrier(d, order) for d in range(line)})

    def carrier(device, order):
        if order < 0:
            return "own"
        k, rises, _ = arrival(device, order)
        if line == 4 and k > 1:
            return "far" if k == 3 else "near" if device in (0, 3) else "middle"
        return f"{'rising' if rises else 'falling'} {k}"

    def choices(order):
        groups = []
        for name in groups_of(order):
            if name == "own":
                parts = own
            elif name in crossing:
                parts = crossing[name]
            else:
                way, k = name.split()
                parts = (rising if way == "rising" else falling)[int(k)]
            groups.append([(part, 0, part.shape[1]) for part in parts])
        return groups

    rows_f = total // 4
    grain = math.gcd(rows_f, shard)
    table = np.zeros((line, 1 + 2 * line), np.int32)
    for d in range(line):
        table[d, 0] = d * local_width
        for order in range(-1, line - 1):
            owner = d if order < 0 else arrival(d, order)[2]
            at = 3 + 2 * order
            table[d, at : at + 2] = groups_of(order).index(carrier(d, order)), owner
    ids = segments[0]
    first_keys = jnp.sum(ids[None, :] < ids[::grain, None], axis=1, dtype=jnp.int32)
    scalars = jnp.concatenate(
        [lax.dynamic_index_in_dim(jnp.asarray(table), member, 0, keepdims=False), first_keys]
    )

    tile_p = min(512, query_width)

    def projection(order, after, low=0, high=None, sums=()):
        groups = choices(order)
        high = len(groups[0]) if high is None else high
        ends = high == len(groups[0])
        groups = [parts[:high] for parts in groups]
        offsets = [0]
        for _, _, columns in groups[0]:
            offsets.append(offsets[-1] + columns)
        places = [[(first, columns) for _, first, columns in parts] for parts in groups]
        width = offsets[high] - offsets[low]
        block, odd = divmod(offsets[low], width)
        assert odd == 0
        operands = [part for parts in groups for part, _, _ in parts]
        in_specs = [ANYWHERE] * len(operands)
        rank_spec = pl.BlockSpec((rank, shard), lambda n, s: (0, 0))
        tile_spec = pl.BlockSpec((shard, tile_p), lambda n, s: (0, n))
        operands += [weight, up_all, down, *sums, *after]
        in_specs += [
            pl.BlockSpec((tile_p, width), lambda n, s: (n, block)),
            pl.BlockSpec((line, rank, local_width), lambda n, s: (0, 0, 0)),
            pl.BlockSpec((rank, tile_p), lambda n, s: (0, n)),
        ]
        in_specs += [tile_spec, rank_spec][: len(sums)] + [ANYWHERE] * len(after)
        out_shape = [
            jax.ShapeDtypeStruct((shard, query_width), bf16 if ends else f32),
            jax.ShapeDtypeStruct((rank, shard), f32),
        ]
        out_specs = [tile_spec, rank_spec]
        scratch = [
            pltpu.VMEM((shard, width), bf16),
            pltpu.SemaphoreType.DMA((high - low,)),
        ]
        if ends:
            out_shape.append(jax.ShapeDtypeStruct((shard, local_width), bf16))
            out_specs.append(
                pl.BlockSpec((shard, local_width * tile_p // query_width), lambda n, s: (0, n))
            )
            scratch.append(pltpu.VMEM((3 * rank, shard), bf16))
            scratch.append(pltpu.VMEM((shard, local_width), bf16))
        return pl.pallas_call(
            functools.partial(
                projection_kernel, (3 + 2 * order, places, low, ends, len(after))
            ),
            grid_spec=pltpu.PrefetchScalarGridSpec(
                num_scalar_prefetch=1,
                grid=(query_width // tile_p,),
                in_specs=in_specs,
                out_specs=out_specs,
                scratch_shapes=scratch,
            ),
            out_shape=out_shape,
            **options(f"projection_{order + 1}_{high}", 18 * width / model_width),
        )(scalars, *operands)

    projected = [projection(-1, [])]
    done_before = projected[0][1]
    if line == 4:
        cross(0, "near", done_before)
        cross(0, "middle", done_before)
        cross(1, "near", done_before)
        cross(1, "middle", done_before)
    else:
        pass_on(done_before)
    if line > 2:
        projected.append(projection(0, [done_before]))
        done_before = projected[1][1]

    ids_column = ids[:, None]
    lanes_f = group * rows_f
    chunk_f = 2 * rows_f if group % 2 == 0 else rows_f

    def row_info(rows, heads):
        pos = jnp.arange(total, dtype=jnp.int32).reshape(total // rows, 1, rows)
        row_ids = ids.reshape(total // rows, 1, rows)
        both = jnp.concatenate([pos, row_ids], axis=1)
        return jnp.tile(both, (1, 1, heads))

    wide = group * HEAD_SIZE
    pins = [crossing["near"][0], crossing["middle"][0]] if line == 4 else []
    key_at, value_at = query_heads, query_heads + kv_heads
    context, lse, rank_portion = pl.pallas_call(
        functools.partial(forward_kernel, grain),
        grid_spec=pltpu.PrefetchScalarGridSpec(
            num_scalar_prefetch=1,
            grid=(4, kv_heads),
            in_specs=[
                pl.BlockSpec((rows_f, wide), lambda b, n, s: (b, n)),
                pl.BlockSpec((total, HEAD_SIZE), lambda b, n, s: (0, key_at + n)),
                pl.BlockSpec((total, HEAD_SIZE), lambda b, n, s: (0, value_at + n)),
                pl.BlockSpec((total, 1), lambda b, n, s: (0, 0)),
                pl.BlockSpec((1, 2, chunk_f), lambda b, n, s: (b, 0, 0)),
                pl.BlockSpec((rank, wide), lambda b, n, s: (0, n)),
                ANYWHERE,
            ]
            + [ANYWHERE] * len(pins),
            out_specs=[
                pl.BlockSpec((rows_f, wide), lambda b, n, s: (b, n)),
                pl.BlockSpec((1, 1, 1, lanes_f), lambda b, n, s: (b, n, 0, 0)),
                pl.BlockSpec((1, rank, rows_f), lambda b, n, s: (b, 0, 0)),
            ],
            scratch_shapes=[
                pltpu.VMEM((total, chunk_f), f32),
                pltpu.VMEM((total, lanes_f), f32),
                pltpu.VMEM((HEAD_SIZE, lanes_f), f32),
            ],
        ),
        out_shape=[
            jax.ShapeDtypeStruct((total, query_width), bf16),
            jax.ShapeDtypeStruct((4, kv_heads, 1, lanes_f), f32),
            jax.ShapeDtypeStruct((4, rank, rows_f), f32),
        ],
        **options("forward", 20, 2),
    )(scalars, packed, packed, packed, ids_column, row_info(rows_f, chunk_f // rows_f), down, done_before, *pins)

    rank_context = rank_portion
    for d in range(1, line):
        route = [(i, (i + d) % line) for i in range(line)]
        rank_context = rank_context + lax.ppermute(rank_portion, "fsdp", route)

    rows = shard
    heads = group
    chunk = rows * max(h for h in range(1, group + 1) if group % h == 0 and (h == 1 or h * rows <= 384))
    normal = (
        lse.reshape(4, query_heads, rows_f // rows, rows)
        .transpose(0, 2, 1, 3)
        .reshape(total // rows, query_heads // heads, 1, heads * rows)
    )
    ranks = (
        rank_context.reshape(4, rank, rows_f // rows, rows)
        .transpose(0, 2, 1, 3)
        .reshape(total // rows, rank, rows)
    )
    info = row_info(rows, chunk // rows)
    tile = heads * HEAD_SIZE
    lanes = heads * rows
    kv_spec = pl.BlockSpec((total, HEAD_SIZE), lambda n, s: (0, n))
    tile_spec = pl.BlockSpec((rows, tile), lambda n, s: (0, n))
    map_spec = pl.BlockSpec((rank, tile), lambda n, s: (0, n))
    rank_spec = pl.BlockSpec((rank, rows), lambda n, s: (0, 0))

    def backward(order, state, source, up_map=None, after=()):
        first = state is None
        last = up_map is not None
        here = 4 + 2 * order
        row_spec = pl.BlockSpec((rows, tile), lambda n, s: (s[here], n))
        ctx_rank_spec = pl.BlockSpec((1, rank, rows), lambda n, s: (s[here], 0, 0))
        operands, in_specs = [], []
        grad, rank_grad, local_columns = source
        if last:
            operands += [local_columns, ranks, up_map]
            in_specs += [tile_spec, ctx_rank_spec, map_spec]
        operands += [
            grad,
            rank_grad,
            packed,
            context,
            packed,
            packed,
            ids_column,
            info,
            normal,
        ]
        in_specs += [
            tile_spec,
            rank_spec,
            row_spec,
            row_spec,
            pl.BlockSpec((total, HEAD_SIZE), lambda n, s: (0, key_at + n)),
            pl.BlockSpec((total, HEAD_SIZE), lambda n, s: (0, value_at + n)),
            pl.BlockSpec((total, 1), lambda n, s: (0, 0)),
            pl.BlockSpec((1, 2, chunk), lambda n, s: (s[here], 0, 0)),
            pl.BlockSpec((1, 1, 1, lanes), lambda n, s: (s[here], n, 0, 0)),
        ]
        aliases = {}
        if not first:
            aliases[1 + len(operands)] = 0
            operands += list(state)
            in_specs += [ANYWHERE, kv_spec, kv_spec, map_spec]
        operands += list(after)
        in_specs += [ANYWHERE] * len(after)
        kv_type = bf16 if last else f32
        out_shape = [
            jax.ShapeDtypeStruct((total, query_width), bf16),
            jax.ShapeDtypeStruct((total, kv_width), kv_type),
            jax.ShapeDtypeStruct((total, kv_width), kv_type),
            jax.ShapeDtypeStruct((rank, query_width), f32),
        ]
        out_specs = [row_spec, kv_spec, kv_spec, map_spec]
        scratch = [
            pltpu.VMEM((total, chunk), f32),
            pltpu.VMEM((3 * rank, rows), bf16),
            pltpu.VMEM((total, HEAD_SIZE), f32),
            pltpu.VMEM((total, HEAD_SIZE), f32),
            pltpu.VMEM((KEY_BLOCK, lanes), bf16),
            pltpu.VMEM((KEY_BLOCK, lanes), bf16),
            pltpu.VMEM((HEAD_SIZE, lanes), f32),
        ]
        if last:
            out_shape.append(jax.ShapeDtypeStruct((rank, local_width), f32))
            out_specs.append(map_spec)
        return pl.pallas_call(
            functools.partial(
                backward_kernel, (here, grain, first, last, len(after))
            ),
            grid_spec=pltpu.PrefetchScalarGridSpec(
                num_scalar_prefetch=1,
                grid=(query_heads // heads,),
                in_specs=in_specs,
                out_specs=out_specs,
                scratch_shapes=scratch,
            ),
            out_shape=out_shape,
            input_output_aliases=aliases,
            **options(f"backward_{order + 1}", 8),
        )(scalars, *operands)

    if line == 4:
        cross(0, "far", lse)
    else:
        pass_on(lse)
    state = backward(-1, None, projected[0])
    for order in range(line - 2):
        if order:
            projected.append(projection(order, [state[3]]))
        pins = [crossing["near"][1]] if line == 4 and order == 0 else []
        state = backward(order, state, projected[order + 1], after=pins)
        if line != 4:
            pass_on(state[3])
        elif order == 0:
            cross(1, "far", state[3])

    sums = projection(line - 2, [state[3]], 0, 1)

    count = line - 1
    up_map = pl.pallas_call(
        functools.partial(up_map_kernel, count),
        grid_spec=pltpu.PrefetchScalarGridSpec(
            num_scalar_prefetch=1,
            grid=(local_width // tile,),
            in_specs=[
                pl.BlockSpec((1, rank, rows), lambda n, s, j=j: (s[2 + 2 * j], 0, 0)) for j in range(count)
            ]
            + [tile_spec] * count
            + [ANYWHERE],
            out_specs=map_spec,
        ),
        out_shape=jax.ShapeDtypeStruct((rank, local_width), f32),
        **options("up_map", 3),
    )(scalars, *([ranks] * count), *[p[2] for p in projected], sums[1])
    end = projection(line - 2, [], 1, 2, sums)
    query_gradient, key_gradient, value_gradient, down_map, up_map = backward(
        line - 2, state, end, up_map
    )
    return (
        query_gradient[None],
        key_gradient[None],
        value_gradient[None],
        down_map[None],
        up_map[None],
    )


def solution(mesh):
    placed = (
        P("pipe", "fsdp", None),
        P("pipe", "fsdp", None),
        P("pipe", None, "fsdp"),
        P("pipe", None, "fsdp"),
        P("pipe", None, "fsdp"),
        P("pipe", None, "fsdp"),
        P("pipe", None, "fsdp"),
        P("pipe", None),
    )
    return jax.shard_map(
        per_device,
        mesh=mesh,
        in_specs=placed,
        out_specs=(
            P("pipe", None, "fsdp"),
            P("pipe", None, "fsdp"),
            P("pipe", None, "fsdp"),
            P("pipe", None, "fsdp"),
            P("pipe", None, "fsdp"),
        ),
        check_vma=False,
    )
```

```python
import functools
import math

import jax
import jax.numpy as jnp
import numpy as np
from jax import lax
from jax.experimental import pallas as pl
from jax.experimental.pallas import tpu as pltpu
from jax.sharding import PartitionSpec as P

HEAD_SIZE = 128
MASKED = -1e30
LOG2E = math.log2(math.e)
VMEM_BYTES = 40 * 2**20
KEY_BLOCK = 192
QKV_AFTER = 1
FLOPS_PER_MICRO = 1.0e9

adapter_scale = 2.0


def dot_nt(a, b):
    return lax.dot_general(a, b, (((1,), (1,)), ((), ())), preferred_element_type=jnp.float32)


def dot_nn(a, b):
    return lax.dot_general(a, b, (((1,), (0,)), ((), ())), preferred_element_type=jnp.float32)


def dot_tn(a, b):
    return lax.dot_general(a, b, (((0,), (0,)), ((), ())), preferred_element_type=jnp.float32)


def three_parts(a):
    high = a.astype(jnp.bfloat16)
    rest = a - high.astype(jnp.float32)
    middle = rest.astype(jnp.bfloat16)
    low = (rest - middle.astype(jnp.float32)).astype(jnp.bfloat16)
    return jnp.concatenate([high, middle, low], axis=0)


def folded(a):
    rows = a.shape[0] // 3
    return a[:rows] + a[rows : 2 * rows] + a[2 * rows :]


def stacked_heads(a):
    count = a.shape[1] // HEAD_SIZE
    return jnp.concatenate(
        [a[:, h * HEAD_SIZE : (h + 1) * HEAD_SIZE] for h in range(count)], axis=0
    )


def key_blocks(first_key, row_start, rows):
    return first_key // KEY_BLOCK, (row_start + rows + KEY_BLOCK - 1) // KEY_BLOCK


def fill_bias(bias_ref, ids_ref, row_info_ref, low, high):
    lanes = bias_ref.shape[1]

    def one(i, _):
        at = pl.multiple_of(i * KEY_BLOCK, KEY_BLOCK)
        key_pos = at + lax.broadcasted_iota(jnp.int32, (KEY_BLOCK, lanes), 0)
        allowed = (key_pos <= row_info_ref[0, 0:1, :]) & (
            ids_ref[pl.ds(at, KEY_BLOCK), :] == row_info_ref[0, 1:2, :]
        )
        bias_ref[pl.ds(at, KEY_BLOCK), :] = jnp.where(allowed, 0.0, MASKED)
        return 0

    lax.fori_loop(low, high, one, 0)


def forward_kernel(
    grain, scalars_ref, q_ref, k_ref, v_ref, ids_ref, row_info_ref, down_ref, *rest
):
    ctx_ref, lse_ref, rank_ref, bias_ref, scores_ref, context_ref = rest[-6:]
    step = pl.program_id(1)
    rows = q_ref.shape[0]
    heads = q_ref.shape[1] // HEAD_SIZE
    row_start = pl.program_id(0) * rows
    first_key = scalars_ref[scalars_ref.shape[0] - k_ref.shape[0] // grain + row_start // grain]
    low, high = key_blocks(first_key, row_start, rows)
    lanes = heads * rows
    chunk = bias_ref.shape[1]

    @pl.when(step == 0)
    def _():
        fill_bias(bias_ref, ids_ref, row_info_ref, low, high)
        rank_ref[...] = jnp.zeros_like(rank_ref)

    stacked = stacked_heads(q_ref[...])

    def weigh(i, carry):
        top, weight = carry
        at = pl.multiple_of(i * KEY_BLOCK, KEY_BLOCK)
        keys = k_ref[pl.ds(at, KEY_BLOCK), :]
        bias = bias_ref[pl.ds(at, KEY_BLOCK), :]
        tops, weights = [], []
        for c in range(0, lanes, chunk):
            scores = dot_nt(keys, stacked[c : c + chunk]) * (LOG2E / math.sqrt(HEAD_SIZE)) + bias
            scores_ref[pl.ds(at, KEY_BLOCK), c : c + chunk] = scores
            old = top[:, c : c + chunk]
            new = jnp.maximum(old, jnp.max(scores, axis=0, keepdims=True))
            tops.append(new)
            weights.append(
                weight[:, c : c + chunk] * jnp.exp2(old - new)
                + jnp.sum(jnp.exp2(scores - new), axis=0, keepdims=True)
            )
        return jnp.concatenate(tops, axis=1), jnp.concatenate(weights, axis=1)

    top, weight = lax.fori_loop(
        low,
        high,
        weigh,
        (jnp.full((1, lanes), 2 * MASKED, jnp.float32), jnp.zeros((1, lanes), jnp.float32)),
    )
    lse = top + jnp.log(weight) * LOG2E
    lse_ref[0, 0] = lse
    context_ref[...] = jnp.zeros_like(context_ref)

    def add_values(i, _):
        at = pl.multiple_of(i * KEY_BLOCK, KEY_BLOCK)
        values = v_ref[pl.ds(at, KEY_BLOCK), :]
        for c in range(0, lanes, chunk):
            scores = scores_ref[pl.ds(at, KEY_BLOCK), c : c + chunk]
            probs = jnp.exp2(scores - lse[:, c : c + chunk]).astype(jnp.bfloat16)
            context_ref[:, c : c + chunk] += dot_tn(values, probs)
        return 0

    lax.fori_loop(low, high, add_values, 0)
    context = context_ref[...].T.astype(jnp.bfloat16)
    for h in range(heads):
        part = context[h * rows : (h + 1) * rows]
        ctx_ref[:, h * HEAD_SIZE : (h + 1) * HEAD_SIZE] = part
        rank_ref[0] += dot_nt(down_ref[:, h * HEAD_SIZE : (h + 1) * HEAD_SIZE], part)


def fetch(choice, groups, x_ref, sems):
    for c, parts in enumerate(groups):

        @pl.when(choice == c)
        def _(parts=parts):
            copies = []
            at = 0
            for p, (part, first, width) in enumerate(parts):
                copies.append(
                    pltpu.make_async_copy(
                        part.at[:, pl.ds(first, width)], x_ref.at[:, pl.ds(at, width)], sems.at[p]
                    )
                )
                at += width
            for copy in copies:
                copy.start()
            for copy in copies:
                copy.wait()


def rank_product(up_ref, x_ref, first_column):
    local = up_ref.shape[2]
    width = x_ref.shape[1]
    total = None
    for j in range(width // local):
        part = dot_nt(up_ref[first_column // local + j], x_ref[:, j * local : (j + 1) * local])
        total = part if total is None else total + part
    return total


def project(x_ref, w_ref, acc):
    width = x_ref.shape[1]
    for at in range(0, width, 4096):
        to = min(at + 4096, width)
        acc = acc + dot_nt(x_ref[:, at:to], w_ref[:, at:to])
    return acc


def rank_term(rank, down):
    return adapter_scale * dot_tn(rank, jnp.concatenate([down, down, down], axis=0))


def projection_kernel(spec, scalars_ref, *refs):
    at_choice, places, before, ends, after = spec
    refs = list(refs)

    def take(count):
        taken = refs[:count]
        del refs[:count]
        return taken

    groups = [
        [(ref, *place) for ref, place in zip(take(len(group)), group)] for group in places
    ]
    first_column = sum(columns for _, columns in places[0][:before])
    w_ref, up_ref, down_ref = take(3)
    if before:
        acc_in, rank_in = take(2)
    take(after)
    out_ref, rank_out = take(2)
    if ends:
        local_out = take(1)[0]
    x_ref, sems = take(2)
    if ends:
        parts_ref, local_ref = take(2)
    step = pl.program_id(0)

    @pl.when(step == 0)
    def _():
        fetch(scalars_ref[at_choice], [parts[before:] for parts in groups], x_ref, sems)
        rank = rank_product(up_ref, x_ref, first_column)
        rank_out[...] = rank + rank_in[...] if before else rank
        if ends:
            parts_ref[...] = three_parts(rank_out[...])
            for c, parts in enumerate(groups):
                at = 0
                for part, first, width in parts:
                    mine = scalars_ref[0] - at

                    @pl.when((scalars_ref[at_choice] == c) & (mine >= 0) & (mine < width))
                    def _(part=part, mine=mine, first=first):
                        copy = pltpu.make_async_copy(
                            part.at[:, pl.ds(pl.multiple_of(mine + first, 128), local_ref.shape[1])],
                            local_ref,
                            sems.at[0],
                        )
                        copy.start()
                        copy.wait()

                    at += width

    if ends:
        begin = rank_term(parts_ref[...], down_ref[...])
        if before:
            begin = begin + acc_in[...]
    else:
        begin = acc_in[...] if before else jnp.zeros(out_ref.shape, jnp.float32)
    out_ref[...] = project(x_ref, w_ref, begin).astype(out_ref.dtype)
    if ends:
        tile = local_out.shape[1]
        local_out[...] = local_ref[:, pl.ds(pl.multiple_of(step * tile, tile), tile)]


def up_map_kernel(count, scalars_ref, *refs):
    ranks = refs[:count]
    columns = refs[count : 2 * count]
    out_ref = refs[2 * count + 1]
    rows_total = sum(c.shape[0] for c in columns)
    scale = adapter_scale / math.sqrt(rows_total * (count + 1) // count)
    total = None
    for rank, column in zip(ranks, columns):
        part = folded(dot_nn(three_parts(rank[0]), column[...]))
        total = part if total is None else total + part
    out_ref[...] = scale * total


def backward_kernel(spec, scalars_ref, *refs):
    here, grain, first, last, after = spec
    refs = list(refs)

    def take(count):
        taken = refs[:count]
        del refs[:count]
        return taken

    if last:
        local_ref, rank_ctx_ref, um_in = take(3)
    grad_ref, rank_in, q_ref, ctx_ref, k_ref, v_ref, ids_ref, row_info_ref, lse_ref = take(9)
    if not first:
        _, dk_in, dv_in, dm_in = take(4)
    take(after)
    dq_ref, dk_ref, dv_ref, dm_ref = take(4)
    if last:
        um_ref = take(1)[0]
    bias_ref, parts_ref, dk_sum, dv_sum, probs_ref, grad_scores_ref, grad_q_ref = take(7)

    step = pl.program_id(0)
    total = k_ref.shape[0]
    rows = q_ref.shape[0]
    heads = q_ref.shape[1] // HEAD_SIZE
    lanes = heads * rows
    chunk = bias_ref.shape[1]
    row_start = scalars_ref[here] * rows
    first_key = scalars_ref[scalars_ref.shape[0] - total // grain + row_start // grain]
    low, high = key_blocks(first_key, row_start, rows)
    gradient_scale = adapter_scale / math.sqrt(total)
    inv_scale = 1.0 / math.sqrt(HEAD_SIZE)

    @pl.when(step == 0)
    def _():
        parts_ref[...] = three_parts(rank_in[...])
        fill_bias(bias_ref, ids_ref, row_info_ref, low, high)

    if first:
        dk_sum[...] = jnp.zeros_like(dk_sum)
        dv_sum[...] = jnp.zeros_like(dv_sum)
    else:
        dk_sum[...] = dk_in[...]
        dv_sum[...] = dv_in[...]
    grad_q_ref[...] = jnp.zeros_like(grad_q_ref)
    queries = stacked_heads(q_ref[...])
    grads = stacked_heads(grad_ref[...])
    delta = jnp.sum(
        (grads.astype(jnp.float32) * stacked_heads(ctx_ref[...]).astype(jnp.float32)).T,
        axis=0,
        keepdims=True,
    )

    def one(i, _):
        at = pl.multiple_of(i * KEY_BLOCK, KEY_BLOCK)
        keys = k_ref[pl.ds(at, KEY_BLOCK), :]
        values = v_ref[pl.ds(at, KEY_BLOCK), :]
        bias = bias_ref[pl.ds(at, KEY_BLOCK), :]
        for c in range(0, lanes, chunk):
            here = slice(c, c + chunk)
            scores = dot_nt(keys, queries[here]) * (LOG2E * inv_scale) + bias
            probs = jnp.exp2(scores - lse_ref[0, 0, :, here])
            grad_probs = dot_nt(values, grads[here])
            probs_ref[:, here] = probs.astype(jnp.bfloat16)
            grad_scores_ref[:, here] = (probs * (grad_probs - delta[:, here])).astype(jnp.bfloat16)
        grad_scores = grad_scores_ref[...]
        dk_sum[pl.ds(at, KEY_BLOCK), :] += dot_nn(grad_scores, queries) * inv_scale
        dv_sum[pl.ds(at, KEY_BLOCK), :] += dot_nn(probs_ref[...], grads)
        grad_q_ref[...] += dot_tn(keys, grad_scores)
        return 0

    lax.fori_loop(low, high, one, 0)
    dk_ref[...] = dk_sum[...].astype(dk_ref.dtype)
    dv_ref[...] = dv_sum[...].astype(dv_ref.dtype)
    grad_q = (grad_q_ref[...] * inv_scale).T.astype(jnp.bfloat16)
    for h in range(heads):
        dq_ref[:, h * HEAD_SIZE : (h + 1) * HEAD_SIZE] = grad_q[h * rows : (h + 1) * rows]

    down_part = gradient_scale * folded(dot_nn(parts_ref[...], ctx_ref[...]))
    dm_ref[...] = down_part if first else dm_in[...] + down_part
    if last:
        um_ref[...] = um_in[...] + gradient_scale * folded(
            dot_nn(three_parts(rank_ctx_ref[0]), local_ref[...])
        )


def options(name, micros, axes=1):
    return dict(
        compiler_params=pltpu.CompilerParams(
            dimension_semantics=("arbitrary",) * axes, vmem_limit_bytes=VMEM_BYTES
        ),
        cost_estimate=pl.CostEstimate(
            flops=int(micros * FLOPS_PER_MICRO), bytes_accessed=1, transcendentals=0
        ),
        name=name,
    )


ANYWHERE = pl.BlockSpec(memory_space=pl.ANY)


def per_device(
    handoff_gradient,
    output_weight,
    adapter_down,
    adapter_up,
    stored_queries,
    stored_keys,
    stored_values,
    segments,
):
    pipe_count = lax.axis_size("pipe")
    line = lax.axis_size("fsdp")
    member = lax.axis_index("fsdp")
    shard = handoff_gradient.shape[1]
    total = shard * line
    model_width = handoff_gradient.shape[2]
    query_width = stored_queries.shape[2]
    kv_width = stored_keys.shape[2]
    rank = adapter_down.shape[1]
    query_heads = query_width // HEAD_SIZE
    kv_heads = kv_width // HEAD_SIZE
    group = query_heads // kv_heads
    local_width = adapter_up.shape[2]
    bf16, f32 = jnp.bfloat16, jnp.float32
    weight = output_weight[0]
    down = adapter_down[0]

    def spread(block):
        blocks = [block]
        for d in range(1, line):
            route = [(i, (i + d) % line) for i in range(line)]
            blocks.append(lax.ppermute(block, "fsdp", route))
        turned = jnp.stack(blocks[::-1] + blocks[::-1])
        return lax.dynamic_slice_in_dim(turned, line - 1 - member, line, 0)

    from_next = [((i + 1) % pipe_count, i) for i in range(pipe_count)]
    mirrored = [(i, pipe_count - 1 - i) for i in range(pipe_count)]
    widths = [model_width // 2, model_width // 2]
    own, at = [], 0
    for width in widths:
        part = handoff_gradient[0, :, at : at + width]
        if own:
            part, _ = lax.optimization_barrier((part, own[-1]))
        own.append(lax.ppermute(part, "pipe", from_next))
        at += width
    packed = jnp.concatenate([stored_queries[0], stored_keys[0], stored_values[0]], axis=1)
    up_all = spread(lax.optimization_barrier((adapter_up[0], own[0]))[0])
    rising, falling = [own], [own]
    crossing = {}

    def after(part, token):
        return part if token is None else lax.optimization_barrier((part, token))[0]

    def pass_on(token):
        k = len(rising)
        if k >= line:
            return
        up_pairs = [(i, i + 1) for i in range(k - 1, line - 1)]
        down_pairs = [(i + 1, i) for i in range(line - k)]
        rising.append([lax.ppermute(after(p, token), "fsdp", up_pairs) for p in rising[-1]])
        falling.append([lax.ppermute(after(p, token), "fsdp", down_pairs) for p in falling[-1]])

    def cross(piece, kind, token, columns=slice(None)):
        routes = {
            "near": [(1, 0), (2, 3)],
            "middle": [(1, 2), (2, 1)],
            "far": [(1, 3), (2, 0)],
        }
        rose, fell = rising[1][piece], falling[1][piece]
        first = member == (2 if kind == "near" else 1)
        part = jnp.where(first, rose, fell)[:, columns]
        crossing.setdefault(kind, []).append(
            lax.ppermute(after(part, token), "fsdp", routes[kind])
        )

    pass_on(None)
    packed, _ = lax.optimization_barrier((packed, own[QKV_AFTER]))
    packed = lax.ppermute(packed, "pipe", mirrored)

    def arrival(device, order):
        found = []
        for k in range(1, line):
            if device >= k:
                found.append((k, True, device - k))
            if device + k < line:
                found.append((k, False, device + k))
        return found[order]

    def groups_of(order):
        if order < 0:
            return ["own"]
        return sorted({carrier(d, order) for d in range(line)})

    def carrier(device, order):
        if order < 0:
            return "own"
        k, rises, _ = arrival(device, order)
        if line == 4 and k > 1:
            return "far" if k == 3 else "near" if device in (0, 3) else "middle"
        return f"{'rising' if rises else 'falling'} {k}"

    def choices(order):
        groups = []
        for name in groups_of(order):
            if name == "own":
                parts = own
            elif name in crossing:
                parts = crossing[name]
            else:
                way, k = name.split()
                parts = (rising if way == "rising" else falling)[int(k)]
            group = [(part, 0, part.shape[1]) for part in parts]
            if line == 4 and order == line - 2 and len(group) == 2:
                half = widths[1] // 2
                group = [group[0], (parts[1], 0, half), (parts[1], half, half)]
            groups.append(group)
        return groups

    rows_f = total // 4
    grain = math.gcd(rows_f, shard)
    table = np.zeros((line, 1 + 2 * line), np.int32)
    for d in range(line):
        table[d, 0] = d * local_width
        for order in range(-1, line - 1):
            owner = d if order < 0 else arrival(d, order)[2]
            at = 3 + 2 * order
            table[d, at : at + 2] = groups_of(order).index(carrier(d, order)), owner
    ids = segments[0]
    first_keys = jnp.sum(ids[None, :] < ids[::grain, None], axis=1, dtype=jnp.int32)
    scalars = jnp.concatenate(
        [lax.dynamic_index_in_dim(jnp.asarray(table), member, 0, keepdims=False), first_keys]
    )

    tile_p = min(512, query_width)

    def projection(order, after, low=0, high=None, sums=()):
        groups = choices(order)
        high = len(groups[0]) if high is None else high
        ends = high == len(groups[0])
        groups = [parts[:high] for parts in groups]
        offsets = [0]
        for _, _, columns in groups[0]:
            offsets.append(offsets[-1] + columns)
        places = [[(first, columns) for _, first, columns in parts] for parts in groups]
        width = offsets[high] - offsets[low]
        block, odd = divmod(offsets[low], width)
        assert odd == 0
        operands = [part for parts in groups for part, _, _ in parts]
        in_specs = [ANYWHERE] * len(operands)
        rank_spec = pl.BlockSpec((rank, shard), lambda n, s: (0, 0))
        tile_spec = pl.BlockSpec((shard, tile_p), lambda n, s: (0, n))
        operands += [weight, up_all, down, *sums, *after]
        in_specs += [
            pl.BlockSpec((tile_p, width), lambda n, s: (n, block)),
            pl.BlockSpec((line, rank, local_width), lambda n, s: (0, 0, 0)),
            pl.BlockSpec((rank, tile_p), lambda n, s: (0, n)),
        ]
        in_specs += [tile_spec, rank_spec][: len(sums)] + [ANYWHERE] * len(after)
        out_shape = [
            jax.ShapeDtypeStruct((shard, query_width), bf16 if ends else f32),
            jax.ShapeDtypeStruct((rank, shard), f32),
        ]
        out_specs = [tile_spec, rank_spec]
        scratch = [
            pltpu.VMEM((shard, width), bf16),
            pltpu.SemaphoreType.DMA((high - low,)),
        ]
        if ends:
            out_shape.append(jax.ShapeDtypeStruct((shard, local_width), bf16))
            out_specs.append(
                pl.BlockSpec((shard, local_width * tile_p // query_width), lambda n, s: (0, n))
            )
            scratch.append(pltpu.VMEM((3 * rank, shard), bf16))
            scratch.append(pltpu.VMEM((shard, local_width), bf16))
        return pl.pallas_call(
            functools.partial(
                projection_kernel, (3 + 2 * order, places, low, ends, len(after))
            ),
            grid_spec=pltpu.PrefetchScalarGridSpec(
                num_scalar_prefetch=1,
                grid=(query_width // tile_p,),
                in_specs=in_specs,
                out_specs=out_specs,
                scratch_shapes=scratch,
            ),
            out_shape=out_shape,
            **options(f"projection_{order + 1}_to_{high}", 18 * width / model_width),
        )(scalars, *operands)

    projected = [projection(-1, [])]
    done_before = projected[0][1]
    if line == 4:
        cross(0, "near", done_before)
        cross(0, "middle", done_before)
        cross(1, "near", done_before)
        cross(1, "middle", done_before)
    else:
        pass_on(done_before)
    if line > 2:
        projected.append(projection(0, [done_before]))
        done_before = projected[1][1]

    ids_column = ids[:, None]
    lanes_f = group * rows_f
    chunk_f = 2 * rows_f if group % 2 == 0 else rows_f

    def row_info(rows, heads):
        pos = jnp.arange(total, dtype=jnp.int32).reshape(total // rows, 1, rows)
        row_ids = ids.reshape(total // rows, 1, rows)
        both = jnp.concatenate([pos, row_ids], axis=1)
        return jnp.tile(both, (1, 1, heads))

    wide = group * HEAD_SIZE
    pins = [crossing["near"][0], crossing["middle"][0]] if line == 4 else []
    key_at, value_at = query_heads, query_heads + kv_heads
    context, lse, rank_portion = pl.pallas_call(
        functools.partial(forward_kernel, grain),
        grid_spec=pltpu.PrefetchScalarGridSpec(
            num_scalar_prefetch=1,
            grid=(4, kv_heads),
            in_specs=[
                pl.BlockSpec((rows_f, wide), lambda b, n, s: (b, n)),
                pl.BlockSpec((total, HEAD_SIZE), lambda b, n, s: (0, key_at + n)),
                pl.BlockSpec((total, HEAD_SIZE), lambda b, n, s: (0, value_at + n)),
                pl.BlockSpec((total, 1), lambda b, n, s: (0, 0)),
                pl.BlockSpec((1, 2, chunk_f), lambda b, n, s: (b, 0, 0)),
                pl.BlockSpec((rank, wide), lambda b, n, s: (0, n)),
                ANYWHERE,
            ]
            + [ANYWHERE] * len(pins),
            out_specs=[
                pl.BlockSpec((rows_f, wide), lambda b, n, s: (b, n)),
                pl.BlockSpec((1, 1, 1, lanes_f), lambda b, n, s: (b, n, 0, 0)),
                pl.BlockSpec((1, rank, rows_f), lambda b, n, s: (b, 0, 0)),
            ],
            scratch_shapes=[
                pltpu.VMEM((total, chunk_f), f32),
                pltpu.VMEM((total, lanes_f), f32),
                pltpu.VMEM((HEAD_SIZE, lanes_f), f32),
            ],
        ),
        out_shape=[
            jax.ShapeDtypeStruct((total, query_width), bf16),
            jax.ShapeDtypeStruct((4, kv_heads, 1, lanes_f), f32),
            jax.ShapeDtypeStruct((4, rank, rows_f), f32),
        ],
        **options("forward", 20, 2),
    )(scalars, packed, packed, packed, ids_column, row_info(rows_f, chunk_f // rows_f), down, done_before, *pins)

    rank_context = rank_portion
    for d in range(1, line):
        route = [(i, (i + d) % line) for i in range(line)]
        rank_context = rank_context + lax.ppermute(rank_portion, "fsdp", route)
        if d == 1:
            begun = rank_context

    rows = shard
    heads = group
    chunk = rows * max(h for h in range(1, group + 1) if group % h == 0 and (h == 1 or h * rows <= 384))
    normal = (
        lse.reshape(4, query_heads, rows_f // rows, rows)
        .transpose(0, 2, 1, 3)
        .reshape(total // rows, query_heads // heads, 1, heads * rows)
    )
    ranks = (
        rank_context.reshape(4, rank, rows_f // rows, rows)
        .transpose(0, 2, 1, 3)
        .reshape(total // rows, rank, rows)
    )
    info = row_info(rows, chunk // rows)
    tile = heads * HEAD_SIZE
    lanes = heads * rows
    kv_spec = pl.BlockSpec((total, HEAD_SIZE), lambda n, s: (0, n))
    tile_spec = pl.BlockSpec((rows, tile), lambda n, s: (0, n))
    map_spec = pl.BlockSpec((rank, tile), lambda n, s: (0, n))
    rank_spec = pl.BlockSpec((rank, rows), lambda n, s: (0, 0))

    def backward(order, state, source, up_map=None, after=()):
        first = state is None
        last = up_map is not None
        here = 4 + 2 * order
        row_spec = pl.BlockSpec((rows, tile), lambda n, s: (s[here], n))
        ctx_rank_spec = pl.BlockSpec((1, rank, rows), lambda n, s: (s[here], 0, 0))
        operands, in_specs = [], []
        grad, rank_grad, local_columns = source
        if last:
            operands += [local_columns, ranks, up_map]
            in_specs += [tile_spec, ctx_rank_spec, map_spec]
        operands += [
            grad,
            rank_grad,
            packed,
            context,
            packed,
            packed,
            ids_column,
            info,
            normal,
        ]
        in_specs += [
            tile_spec,
            rank_spec,
            row_spec,
            row_spec,
            pl.BlockSpec((total, HEAD_SIZE), lambda n, s: (0, key_at + n)),
            pl.BlockSpec((total, HEAD_SIZE), lambda n, s: (0, value_at + n)),
            pl.BlockSpec((total, 1), lambda n, s: (0, 0)),
            pl.BlockSpec((1, 2, chunk), lambda n, s: (s[here], 0, 0)),
            pl.BlockSpec((1, 1, 1, lanes), lambda n, s: (s[here], n, 0, 0)),
        ]
        aliases = {}
        if not first:
            aliases[1 + len(operands)] = 0
            operands += list(state)
            in_specs += [ANYWHERE, kv_spec, kv_spec, map_spec]
        operands += list(after)
        in_specs += [ANYWHERE] * len(after)
        kv_type = bf16 if last else f32
        out_shape = [
            jax.ShapeDtypeStruct((total, query_width), bf16),
            jax.ShapeDtypeStruct((total, kv_width), kv_type),
            jax.ShapeDtypeStruct((total, kv_width), kv_type),
            jax.ShapeDtypeStruct((rank, query_width), f32),
        ]
        out_specs = [row_spec, kv_spec, kv_spec, map_spec]
        scratch = [
            pltpu.VMEM((total, chunk), f32),
            pltpu.VMEM((3 * rank, rows), bf16),
            pltpu.VMEM((total, HEAD_SIZE), f32),
            pltpu.VMEM((total, HEAD_SIZE), f32),
            pltpu.VMEM((KEY_BLOCK, lanes), bf16),
            pltpu.VMEM((KEY_BLOCK, lanes), bf16),
            pltpu.VMEM((HEAD_SIZE, lanes), f32),
        ]
        if last:
            out_shape.append(jax.ShapeDtypeStruct((rank, local_width), f32))
            out_specs.append(map_spec)
        return pl.pallas_call(
            functools.partial(
                backward_kernel, (here, grain, first, last, len(after))
            ),
            grid_spec=pltpu.PrefetchScalarGridSpec(
                num_scalar_prefetch=1,
                grid=(query_heads // heads,),
                in_specs=in_specs,
                out_specs=out_specs,
                scratch_shapes=scratch,
            ),
            out_shape=out_shape,
            input_output_aliases=aliases,
            **options(f"backward_{order + 1}", 8),
        )(scalars, *operands)

    if line == 4:
        cross(0, "far", lse)
    else:
        pass_on(lse)
    state = backward(-1, None, projected[0])
    for order in range(line - 2):
        if order:
            projected.append(projection(order, [state[3]]))
        pins = [crossing["near"][1] if order == 0 else begun] if line == 4 else []
        state = backward(order, state, projected[order + 1], after=pins)
        if line != 4:
            pass_on(state[3])
        elif order == 0:
            half = widths[1] // 2
            cross(1, "far", state[3], slice(0, half))
            cross(1, "far", state[3], slice(half, None))

    last_piece = len(choices(line - 2)[0]) - 1
    sums = ()
    for p in range(last_piece):
        sums = projection(line - 2, [state[3]], p, p + 1, sums)

    count = line - 1
    up_map = pl.pallas_call(
        functools.partial(up_map_kernel, count),
        grid_spec=pltpu.PrefetchScalarGridSpec(
            num_scalar_prefetch=1,
            grid=(local_width // tile,),
            in_specs=[
                pl.BlockSpec((1, rank, rows), lambda n, s, j=j: (s[2 + 2 * j], 0, 0)) for j in range(count)
            ]
            + [tile_spec] * count
            + [ANYWHERE],
            out_specs=map_spec,
        ),
        out_shape=jax.ShapeDtypeStruct((rank, local_width), f32),
        **options("up_map", 3),
    )(scalars, *([ranks] * count), *[p[2] for p in projected], sums[1])
    end = projection(line - 2, [], last_piece, None, sums)
    query_gradient, key_gradient, value_gradient, down_map, up_map = backward(
        line - 2, state, end, up_map
    )
    return (
        query_gradient[None],
        key_gradient[None],
        value_gradient[None],
        down_map[None],
        up_map[None],
    )


def solution(mesh):
    placed = (
        P("pipe", "fsdp", None),
        P("pipe", "fsdp", None),
        P("pipe", None, "fsdp"),
        P("pipe", None, "fsdp"),
        P("pipe", None, "fsdp"),
        P("pipe", None, "fsdp"),
        P("pipe", None, "fsdp"),
        P("pipe", None),
    )
    return jax.shard_map(
        per_device,
        mesh=mesh,
        in_specs=placed,
        out_specs=(
            P("pipe", None, "fsdp"),
            P("pipe", None, "fsdp"),
            P("pipe", None, "fsdp"),
            P("pipe", None, "fsdp"),
            P("pipe", None, "fsdp"),
        ),
        check_vma=False,
    )
```
